32 devices in a mesh: dp: 2 (over x), tile: 16 (over z, y, core).
Axes of the slice: x: 2, y: 2, z: 4, core: 2. Of those that a mesh axis runs over, the one named last changes fastest.
Arguments:
- grad_out: bfloat16 [2, 64, 640, 512], P('dp', 'tile'), may hold values from -6 to 6
- bev_act: bfloat16 [2, 64, 640, 512], P('dp', 'tile'), may hold values from -6 to 6
- conv_weight: bfloat16 [512, 3, 3, 512], replicated, may hold values from -0.09375 to 0.09375
- img_in: bfloat16 [2, 8192, 512], P('dp', 'tile'), may hold values from -6 to 6
- backbone_weight: bfloat16 [512, 512], replicated, may hold values from -0.25 to 0.25
- route: int32 [2, 640], P('dp'), may hold values from 0 to 63, as said below
- offsets: int32 [2, 40960], P('dp', 'tile'), may hold values from 0 to 62
- frac_x: int32 [2, 40960], P('dp', 'tile'), may hold values from 0 to 255
- frac_y: int32 [2, 40960], P('dp', 'tile'), may hold values from 0 to 255
Outputs:
- image_grad: bfloat16 [2, 8192, 512], P('dp', 'tile')
- conv_grad: bfloat16 [512, 3, 3, 512], replicated
- backbone_grad: bfloat16 [512, 512], replicated
The draws below stay inside these ranges and needn't reach their ends.
Inputs may be any that keep to these rules, and one draw needn't show every extreme that they name: `route`: owner of image block id is id // 4. Among the 40 ground blocks k * 40 to k * 40 + 39 of one sample, at most 5 have sources with one owner; in every sample some owner has exactly 5 such blocks from every device.
All inputs are finite; a program needn't handle non-finite values.
Results may differ from the reference program's by a relative error of at most 0.0073.
Values may be sent and summed in bfloat16 or wider, within the bound.
No kernel may reach another device: no remote copies, remote signals or barrier semaphores. Data moves between devices by JAX's collectives and lax.ppermute only.
A program may use at most 192 MiB of HBM per device.

```python
import math
import jax
import jax.numpy as jnp
from jax import lax

C = 512
BW = 640
IB = 4
BLK = 64
IMGW = 64
BATCH = 2
NBR = 64
NB = 40
TOTB = 640
CAP = 5
IMGB = 64
PIX = 8192
CELLS = 81920
PIXELS = 16384
N_TILE = 16


def draw_route(key, part):
    slot_total = N_TILE * CAP

    def one_sample(sample_key):
        favored = jax.random.randint(jax.random.fold_in(sample_key, 7), (), 0, N_TILE)

        def one_device(device_key):
            perm = jax.random.permutation(jax.random.fold_in(device_key, 1), slot_total)
            owner = perm // CAP
            edge = (perm == 0) | (perm == (N_TILE - 1) * CAP)
            score = jnp.where(owner == favored, 0, jnp.where(edge, 1, 2)).astype(jnp.int32)
            order = jnp.argsort(score, stable=True)
            chosen = perm[order][:NB]
            local = jax.random.randint(jax.random.fold_in(device_key, 3), (NB,), 0, IB)
            local = jnp.where(chosen == 0, 0, jnp.where(chosen == (N_TILE - 1) * CAP, IB - 1, local))
            ids = (chosen // CAP * IB + local).astype(jnp.int32)
            return jax.random.permutation(jax.random.fold_in(device_key, 5), ids)
        device_keys = jax.random.split(jax.random.fold_in(sample_key, 11), N_TILE)
        return jax.vmap(one_device)(device_keys).reshape(-1)
    sample_keys = jax.random.split(jax.random.fold_in(key, 13), BATCH)
    return jax.vmap(one_sample)(sample_keys).astype(jnp.int32)


def place_ends(drawn, own_key, least, largest):
    longest = drawn.shape.index(max(drawn.shape))
    spots = []
    for shift in (0, 1):
        where = [jax.random.randint(jax.random.fold_in(own_key, axis), (), 0, length) for axis, length in enumerate(drawn.shape)]
        where[longest] = (where[longest] + shift) % drawn.shape[longest]
        spots.append(tuple(where))
    return drawn.at[spots[0]].set(least).at[spots[1]].set(largest)


def with_spikes(values, rng, source, target, parts, factor):
    def block_of(axis_at):
        return (jnp.arange(values.shape[axis_at]) // (values.shape[axis_at] // parts)).reshape((-1,) + (1,) * (values.ndim - 1 - axis_at))

    first = jax.random.permutation(rng, parts)[block_of(target)]
    far = (block_of(target) + parts // 2) % parts
    return jnp.where((block_of(source) == first) | (block_of(source) == far), factor * values, values)


def shard_levels(stream_key, extent, shards, least, largest):
    def one(dim, shards_of):
        steps = jax.random.uniform(jax.random.fold_in(jax.random.fold_in(stream_key, 6), dim), (shards_of,), jnp.float32, least / len(shards), largest / len(shards))
        return jnp.repeat(jnp.exp(steps), extent[dim] // shards_of).reshape((-1,) + (1,) * (len(extent) - dim - 1))

    gain = one(*shards[0])
    for cut in shards[1:]:
        gain = gain * one(*cut)
    return gain


def normal_values(stream_key, shape, scale, reach, shards=(), kind=jnp.bfloat16):
    entries = jax.random.normal(stream_key, shape, jnp.float32) * scale
    if len(shards) > 0:
        entries = shard_levels(stream_key, shape, shards, -0.22, 0.18) * entries
    return jnp.clip(entries, min=-reach, max=reach).astype(kind)


def noise_with(stream_key, dims, deviation, reach, cuts, heavy, kind=jnp.bfloat16):
    drawn = deviation * jax.random.normal(stream_key, dims, jnp.float32)
    if cuts:
        drawn = drawn * shard_levels(stream_key, dims, cuts, -0.22, 0.18)
    return jnp.clip(with_spikes(drawn, jax.random.fold_in(stream_key, 3), *heavy), -reach, reach).astype(kind)


def setup_inputs(seed: int = 0) -> dict:
    key_list = jax.random.split(jax.random.key(seed), 10)
    return {
        "grad_out": normal_values(key_list[0], (BATCH, NBR, BW, C), 1.0, 6.0, ((0, 2), (1, 16))),
        "bev_act": noise_with(key_list[1], (BATCH, NBR, BW, C), 1.0, 6.0, ((0, 2), (1, 16)), (1, 3, 16, 2.0)),
        "conv_weight": normal_values(key_list[2], (C, 3, 3, C), (9 * C) ** -0.5, 0.09375),
        "img_in": noise_with(key_list[3], (BATCH, PIX, C), 1.0, 6.0, ((0, 2), (1, 16)), (1, 2, 16, 2.0)),
        "backbone_weight": normal_values(key_list[4], (C, C), C ** -0.5, 0.25),
        "route": draw_route(jax.random.fold_in(key_list[9], 71), 0),
        "offsets": place_ends(jax.random.randint(key_list[6], (BATCH, NBR * BW), 0, IMGW - 1), jax.random.fold_in(key_list[6], 1), 0, (IMGW - 1) - 1).astype(jnp.int32),
        "frac_x": place_ends(jax.random.randint(key_list[7], (BATCH, NBR * BW), 0, 256), jax.random.fold_in(key_list[7], 1), 0, 255).astype(jnp.int32),
        "frac_y": place_ends(jax.random.randint(key_list[8], (BATCH, NBR * BW), 0, 256), jax.random.fold_in(key_list[8], 1), 0, 255).astype(jnp.int32),
    }


def make_band(offsets, frac_x, frac_y, blocks, width):
    columns = lax.broadcasted_iota(jnp.int32, (1, 1, width), 2)
    shaped = offsets.reshape(blocks, -1, 1)
    right_w = frac_x.reshape(blocks, -1, 1).astype(jnp.float32) / 256.0
    lower_w = frac_y.reshape(blocks, -1, 1).astype(jnp.float32) / 256.0
    across = jnp.where(columns == shaped, 1.0 - right_w, 0.0) + jnp.where(columns == shaped + 1, right_w, 0.0)
    return jnp.concatenate([(1.0 - lower_w) * across, lower_w * across], axis=2).astype(jnp.bfloat16)

def silu_slope(value):
    sigma = jax.nn.sigmoid(value)
    return sigma * (1.0 + value * (1.0 - sigma))

def reference(grad_out, bev_act, conv_weight, img_in, backbone_weight, route, offsets, frac_x, frac_y):
    conv_total = jnp.zeros((C, 3, 3, C), jnp.float32)
    backbone_total = jnp.zeros((C, C), jnp.float32)
    images = []
    for sample in range(BATCH):
        pad_spec = ((1, 1), (1, 1), (0, 0))
        out_frame = jnp.pad(grad_out[sample], pad_spec)
        act_frame = jnp.pad(bev_act[sample], pad_spec)
        center = grad_out[sample].reshape(-1, C)
        bev_sum = jnp.zeros((NBR * BW, C), jnp.float32)
        for row_tap in range(3):
            for col_tap in range(3):
                shifted = out_frame[2 - row_tap:2 - row_tap + NBR, 2 - col_tap:2 - col_tap + BW].reshape(-1, C)
                bev_sum = bev_sum + jnp.dot(shifted, conv_weight[:, row_tap, col_tap, :].T, preferred_element_type=jnp.float32)
                moved = act_frame[row_tap:row_tap + NBR, col_tap:col_tap + BW].reshape(-1, C)
                term = jnp.dot(moved.T, center, preferred_element_type=jnp.float32)
                conv_total = conv_total.at[:, row_tap, col_tap, :].add(term)
        bev_grad = bev_sum.astype(jnp.bfloat16)
        blocks = bev_grad.reshape(TOTB, BLK, C)
        band = make_band(offsets[sample], frac_x[sample], frac_y[sample], TOTB, IMGW)
        pieces = jnp.einsum('kmp,kmc->kpc', band.astype(jnp.float32), blocks.astype(jnp.float32)).astype(jnp.bfloat16)
        feature_grad = jax.ops.segment_sum(pieces.astype(jnp.float32), route[sample], num_segments=IMGB).reshape(PIX, C)
        image = img_in[sample]
        pre = jnp.dot(image, backbone_weight, preferred_element_type=jnp.float32)
        scaled = (feature_grad * silu_slope(pre)).astype(jnp.bfloat16)
        images.append(jnp.dot(scaled, backbone_weight.T, preferred_element_type=jnp.float32).astype(jnp.bfloat16))
        backbone_total = backbone_total + jnp.dot(image.T, scaled, preferred_element_type=jnp.float32)
    conv_grad = (conv_total * (1.0 / math.sqrt(CELLS))).astype(jnp.bfloat16)
    backbone_grad = (backbone_total * (1.0 / math.sqrt(PIXELS))).astype(jnp.bfloat16)
    return (jnp.stack(images), conv_grad, backbone_grad)
```

```python
import functools
import math

import jax
import jax.numpy as jnp
from jax import lax
from jax.experimental import pallas as pl
from jax.experimental.pallas import tpu as pltpu
from jax.sharding import PartitionSpec as P

BLK = 64
IMGW = 64
GROUP = 4
VMEM_BYTES = 56 * 1024 * 1024
F32 = jnp.float32
BF16 = jnp.bfloat16
VMEM = pl.BlockSpec(memory_space=pltpu.VMEM)
SMEM = pl.BlockSpec(memory_space=pltpu.SMEM)
ANY = pl.BlockSpec(memory_space=pl.ANY)


def params(**extra):
    return pltpu.CompilerParams(vmem_limit_bytes=VMEM_BYTES, **extra)


def cost(flops, nbytes):
    return pl.CostEstimate(flops=int(flops), bytes_accessed=int(nbytes), transcendentals=0)


def nt_dot(a, b):
    return lax.dot_general(a, b, (((1,), (1,)), ((), ())), preferred_element_type=F32)


def column_shift(value, by):
    if by == 0:
        return value
    length = value.shape[0]
    place = lax.broadcasted_iota(jnp.int32, value.shape, 0)
    edge = length - 1 if by > 0 else 0
    return jnp.where(place == edge, 0.0, pltpu.roll(value, (-by) % length, 0))


def bev_inner_kernel(g_ref, w_ref, inner_ref, edge_ref, acc_ref):
    rows = g_ref.shape[0]
    step = pl.program_id(0)

    def row_terms(u, taps, j, first):
        lhs = jnp.concatenate([g_ref[u - i + 1] for i in taps], axis=1)
        rhs = jnp.concatenate([w_ref[i, 0] for i in taps], axis=1)
        term = column_shift(nt_dot(lhs, rhs), 1 - j)
        if first:
            acc_ref[u] = term
        else:
            acc_ref[u] = acc_ref[u] + term

    for order, j in enumerate((1, 0, 2)):
        @pl.when(step == order)
        def _(j=j, order=order):
            row_terms(0, (0, 1), j, order == 0)
            row_terms(rows - 1, (1, 2), j, order == 0)

            @pl.loop(1, rows - 1)
            def _(u):
                row_terms(u, (0, 1, 2), j, order == 0)

    @pl.when(step == 2)
    def _():
        edge_ref[0] = acc_ref[0]
        edge_ref[1] = acc_ref[rows - 1]

        @pl.loop(1, rows - 1)
        def _(u):
            inner_ref[u - 1] = acc_ref[u].astype(BF16)


def col_tap(step):
    return jnp.where(step == 0, 1, jnp.where(step == 1, 0, 2))


def bev_inner(grad, weight):
    rows, cols, chans = grad.shape
    whole = lambda *shape: pl.BlockSpec(shape, lambda s: (0,) * len(shape))
    return pl.pallas_call(
        bev_inner_kernel,
        grid=(3,),
        in_specs=[
            whole(rows, cols, chans),
            pl.BlockSpec((3, 1, chans, chans), lambda s: (0, col_tap(s), 0, 0)),
        ],
        out_specs=[whole(rows - 2, cols, chans), whole(2, cols, chans)],
        out_shape=[
            jax.ShapeDtypeStruct((rows - 2, cols, chans), BF16),
            jax.ShapeDtypeStruct((2, cols, chans), F32),
        ],
        scratch_shapes=[pltpu.VMEM((rows, cols, chans), F32)],
        compiler_params=params(),
        cost_estimate=cost(2 * (3 * rows - 2) * 3 * cols * chans * chans, 2 * (rows * cols * chans * 2 + 9 * chans * chans)),
        name="bev_inner",
    )(grad, weight)


def bev_edge_kernel(edge_ref, low_ref, high_ref, wl_ref, wh_ref, out_ref, acc_ref):
    step = pl.program_id(0)
    for order, j in enumerate((1, 0, 2)):
        @pl.when(step == order)
        def _(j=j, order=order):
            for side, (halo, w) in enumerate(((low_ref, wl_ref), (high_ref, wh_ref))):
                term = column_shift(nt_dot(halo[...], w[0, 0]), 1 - j)
                base = edge_ref[side] if order == 0 else acc_ref[side]
                if order == 2:
                    out_ref[side] = (base + term).astype(BF16)
                else:
                    acc_ref[side] = base + term


def bev_edge(edge, low, high, weight):
    _, cols, chans = edge.shape
    whole = lambda *shape: pl.BlockSpec(shape, lambda s: (0,) * len(shape))
    return pl.pallas_call(
        bev_edge_kernel,
        grid=(3,),
        in_specs=[
            whole(2, cols, chans),
            whole(cols, chans),
            whole(cols, chans),
            pl.BlockSpec((1, 1, chans, chans), lambda s: (2, col_tap(s), 0, 0)),
            pl.BlockSpec((1, 1, chans, chans), lambda s: (0, col_tap(s), 0, 0)),
        ],
        out_specs=whole(2, cols, chans),
        out_shape=jax.ShapeDtypeStruct((2, cols, chans), BF16),
        scratch_shapes=[pltpu.VMEM((2, cols, chans), F32)],
        compiler_params=params(),
        cost_estimate=cost(2 * 6 * cols * chans * chans, 2 * (8 * cols * chans + 6 * chans * chans)),
        name="bev_edge",
    )(edge, low, high, weight, weight)


def turn_kernel(parts, order_ref, a_ref, out_ref, wide_ref):
    chans, cols = wide_ref.shape
    size = chans // parts
    flat = a_ref[0].astype(F32).T
    place = lax.broadcasted_iota(jnp.int32, flat.shape, 1)
    for j in range(3):
        if j == 0:
            moved = jnp.where(place == 0, 0.0, pltpu.roll(flat, 1, 1))
        elif j == 1:
            moved = flat
        else:
            moved = jnp.where(place == cols - 1, 0.0, pltpu.roll(flat, cols - 1, 1))
        wide_ref[...] = moved

        for s in range(parts):
            source = pl.multiple_of(order_ref[s] * size, size)
            out_ref[j, s * size : (s + 1) * size, :] = wide_ref[pl.ds(source, size), :].astype(BF16)


def turn(act, order):
    rows, cols, chans = act.shape
    parts = order.shape[0]
    return pl.pallas_call(
        functools.partial(turn_kernel, parts),
        grid=(rows,),
        in_specs=[SMEM, pl.BlockSpec((1, cols, chans), lambda u: (u, 0, 0))],
        out_specs=pl.BlockSpec((3, chans, cols), lambda u: (0, 0, u)),
        out_shape=jax.ShapeDtypeStruct((3, chans, rows * cols), BF16),
        scratch_shapes=[pltpu.VMEM((chans, cols), F32)],
        compiler_params=params(),
        cost_estimate=cost(0, 16 * rows * cols * chans),
        name="turn",
    )(order, act)


def wgrad_kernel(taps, cols, a_ref, g_ref, low_ref, high_ref, keep_ref, send_ref):
    step = pl.program_id(0)
    half = pl.program_id(1)
    total = a_ref.shape[2]

    def product(tap):
        a = a_ref[0]
        g = g_ref[...]
        if tap == 1:
            return jnp.dot(a, g, preferred_element_type=F32)
        if tap == 0:
            return jnp.dot(a[:, : total - cols], g[cols:], preferred_element_type=F32) + jnp.dot(
                a[:, total - cols :], high_ref[...], preferred_element_type=F32
            )
        return jnp.dot(a[:, cols:], g[: total - cols], preferred_element_type=F32) + jnp.dot(
            a[:, :cols], low_ref[...], preferred_element_type=F32
        )

    for place, tap in enumerate(taps):
        @pl.when(step // 3 == place)
        def _(tap=tap):
            term = product(tap).astype(BF16)

            @pl.when(half == 0)
            def _():
                send_ref[0] = term

            @pl.when(half == 1)
            def _():
                keep_ref[0] = term


def wgrad(turned, grad, low, high, taps):
    rows, cols, chans = grad.shape
    flat = grad.reshape(rows * cols, chans)
    count = 3 * len(taps)
    half_rows = chans // 2
    whole = lambda *shape: pl.BlockSpec(shape, lambda t, h: (0,) * len(shape))
    in_specs = [
        pl.BlockSpec((1, half_rows, rows * cols), lambda t, h: (t % 3, 1 - h, 0)),
        whole(rows * cols, chans),
    ]
    operands = [turned, flat]
    if taps == (1,):
        kernel = lambda a, g, keep, send: wgrad_kernel(taps, cols, a, g, None, None, keep, send)
    else:
        kernel = functools.partial(wgrad_kernel, taps, cols)
        in_specs += [whole(cols, chans), whole(cols, chans)]
        operands += [low, high]
    half_spec = pl.BlockSpec((1, half_rows, chans), lambda t, h: (t, 0, 0))
    shape = jax.ShapeDtypeStruct((count, half_rows, chans), BF16)
    return pl.pallas_call(
        kernel,
        grid=(count, 2),
        in_specs=in_specs,
        out_specs=[half_spec, half_spec],
        out_shape=[shape, shape],
        compiler_params=params(),
        cost_estimate=cost(2 * count * rows * cols * chans * chans, 2 * (4 * rows * cols * chans + count * chans * chans)),
        name="wgrad",
    )(*operands)


def fold_kernel(keep_ref, recv_ref, first_ref, second_ref):
    cut = first_ref.shape[1]
    first_ref[...] = (keep_ref[:, :cut].astype(F32) + recv_ref[:, :cut].astype(F32)).astype(BF16)
    second_ref[...] = (keep_ref[:, cut:].astype(F32) + recv_ref[:, cut:].astype(F32)).astype(BF16)


def fold(keep, recv):
    n, m = keep.shape[:2]
    rest = keep.shape[2:]
    block = pl.BlockSpec((1, m) + rest, lambda t: (t,) + (0,) * (1 + len(rest)))
    half = pl.BlockSpec((1, m // 2) + rest, lambda t: (t,) + (0,) * (1 + len(rest)))
    shape = jax.ShapeDtypeStruct((n, m // 2) + rest, BF16)
    return pl.pallas_call(
        fold_kernel,
        grid=(n,),
        in_specs=[block, block],
        out_specs=[half, half],
        out_shape=[shape, shape],
        compiler_params=params(),
        cost_estimate=cost(0, 6 * keep.size),
        name="fold",
    )(keep, recv)


def pieces_kernel(
    plan, info_ref, route_ref, off_ref, fx_ref, fy_ref, *refs
):
    own_blocks, per, tile_bits, edge = plan
    sources = refs[:4]
    outs = refs[4:8]
    blocks_ref, acc_ref, count_ref, list_ref, sems = refs[8:]
    copies = []
    start = 0
    for n, source in enumerate(sources):
        size = source.shape[0]
        copies.append(pltpu.make_async_copy(source, blocks_ref.at[pl.ds(start, size)], sems.at[n]))
        start += size
    for copy in copies:
        copy.start()
    tile = info_ref[0]
    core = tile & 1
    slots = outs[0].shape[0] * 2
    half_per = outs[0].shape[1]
    wide = 2 * own_blocks
    inner = own_blocks - 2 * edge

    @pl.loop(0, slots * per)
    def _(n):
        count_ref[n] = 0

    @pl.loop(0, wide)
    def _(n):
        other = n // own_blocks
        k = n - other * own_blocks
        ident = route_ref[(tile ^ other) * own_blocks + k]
        owner = ident // per
        local = ident - owner * per
        away = (owner ^ tile) >> 1

        @pl.when(((owner ^ tile) & 1) == 0)
        def _():
            place = slot_of(away, core, tile_bits)
            at = place * per + local
            have = count_ref[at]
            list_ref[at * wide + have] = n
            count_ref[at] = have + 1

    for copy in copies:
        copy.wait()

    lanes = lax.broadcasted_iota(jnp.int32, (1, 2 * BLK), 1)
    low_lane = lanes < BLK

    def group_product(at, first, have):
        picked = []
        for g in range(GROUP):
            there = first + g < have
            n = jnp.where(there, list_ref[at * wide + jnp.minimum(first + g, wide - 1)], 0)
            other = n // own_blocks
            k = n - other * own_blocks
            spot = jnp.where(
                k < edge, inner + k, jnp.where(k >= own_blocks - edge, inner + k - inner, k - edge)
            )
            picked.append((there, n, other * own_blocks + spot))
        rhs = jnp.concatenate([blocks_ref[spot] for _, _, spot in picked], axis=0)

        def lane_row(ref):
            halves = []
            for p in range(0, GROUP, 2):
                a = ref[pl.ds(picked[p][1], 1), :]
                b = ref[pl.ds(picked[p + 1][1], 1), :]
                halves.append(jnp.where(low_lane, a, b))
            return jnp.concatenate(halves, axis=1)

        valid = jnp.concatenate(
            [
                jnp.where(
                    low_lane,
                    jnp.where(picked[p][0], 1.0, 0.0),
                    jnp.where(picked[p + 1][0], 1.0, 0.0),
                )
                for p in range(0, GROUP, 2)
            ],
            axis=1,
        ).astype(F32)
        left = lane_row(off_ref)
        right_w = lane_row(fx_ref).astype(F32) / 256.0
        lower_w = lane_row(fy_ref).astype(F32) / 256.0
        column = lax.broadcasted_iota(jnp.int32, (IMGW, GROUP * BLK), 0)
        across = jnp.where(column == left, 1.0 - right_w, 0.0) + jnp.where(
            column == left + 1, right_w, 0.0
        )
        band = jnp.concatenate(
            [((1.0 - lower_w) * valid) * across, (lower_w * valid) * across], axis=0
        ).astype(BF16)
        return jnp.dot(band, rhs, preferred_element_type=F32)

    def fill(out, place, local, inside):
        at = place * per + local
        have = count_ref[at]
        value = group_product(at, 0, have)
        out[inside[0], inside[1]] = value.astype(BF16)

        @pl.when(have > GROUP)
        def _():
            acc_ref[...] = value

            @pl.loop(1, (have + GROUP - 1) // GROUP)
            def _(m):
                acc_ref[...] = acc_ref[...] + group_product(at, m * GROUP, have)

            out[inside[0], inside[1]] = acc_ref[...].astype(BF16)

    for chunk in range(2):
        for half in (1, 0):
            out = outs[2 * chunk + half]

            @pl.loop(0, (slots // 2) * half_per, unroll=2)
            def _(n, out=out, half=half, chunk=chunk):
                place = n // half_per
                local = n - place * half_per
                fill(out, half * (slots // 2) + place, chunk * half_per + local, (place, local))


def swap_low_bits(value):
    return (value & ~3) | ((value & 1) << 1) | ((value >> 1) & 1)


def slot_of(away, core, bits):
    place = 0
    first = jnp.where((core == 1) & (bits >= 2), swap_low_bits(away), away)
    for n in range(bits):
        place = place | (((first >> n) & 1) << (bits - 1 - n))
    return place


def warp_pieces(info, route, off, fx, fy, sources, tiles, per, edge):
    own = sources[0].shape[0] + sources[1].shape[0]
    chans = sources[0].shape[2]
    bits = int(math.log2(tiles)) - 1
    slots = tiles // 2
    shape = jax.ShapeDtypeStruct((slots // 2, per // 2, 2 * IMGW, chans), BF16)
    return pl.pallas_call(
        functools.partial(pieces_kernel, (own, per, bits, edge)),
        in_specs=[SMEM, SMEM, VMEM, VMEM, VMEM] + [ANY] * 4,
        out_specs=[VMEM] * 4,
        out_shape=[shape] * 4,
        scratch_shapes=[
            pltpu.VMEM((2 * own, BLK, chans), BF16),
            pltpu.VMEM((2 * IMGW, chans), F32),
            pltpu.SMEM((slots * per,), jnp.int32),
            pltpu.SMEM((slots * per * 2 * own,), jnp.int32),
            pltpu.SemaphoreType.DMA((4,)),
        ],
        compiler_params=params(),
        cost_estimate=cost(
            2 * slots * per * 2 * IMGW * GROUP * BLK * chans, 2 * (own * 2 * BLK * chans + slots * per * 2 * IMGW * chans)
        ),
        name="warp_pieces",
    )(info, route, off, fx, fy, *sources)


def slope_kernel(order_ref, img_ref, w_ref, slope_ref, turned_ref, wide_ref):
    value = jnp.dot(img_ref[...], w_ref[...], preferred_element_type=F32)
    sigma = jax.nn.sigmoid(value)
    slope_ref[...] = sigma * (1.0 + value * (1.0 - sigma))
    wide_ref[...] = img_ref[...].astype(F32).T
    parts = order_ref.shape[0]
    size = wide_ref.shape[0] // parts
    for s in range(parts):
        source = pl.multiple_of(order_ref[s] * size, size)
        turned_ref[s * size : (s + 1) * size, :] = wide_ref[pl.ds(source, size), :].astype(BF16)


def image_slope(order, image, weight):
    pixels, chans = image.shape
    return pl.pallas_call(
        slope_kernel,
        in_specs=[SMEM, VMEM, VMEM],
        out_specs=[VMEM, VMEM],
        out_shape=[
            jax.ShapeDtypeStruct((pixels, chans), F32),
            jax.ShapeDtypeStruct((chans, pixels), BF16),
        ],
        scratch_shapes=[pltpu.VMEM((chans, pixels), F32)],
        compiler_params=params(),
        cost_estimate=cost(2 * pixels * chans * chans, 10 * pixels * chans),
        name="image_slope",
    )(order, image, weight)


def image_kernel(ka, ra, kb, rb, slope_ref, turned_ref, w_ref, img_out, keep_ref, send_ref):
    half = ka.shape[0]
    feature = jnp.concatenate(
        [ka[...].astype(F32) + ra[...].astype(F32), kb[...].astype(F32) + rb[...].astype(F32)], axis=0
    )
    scaled = (feature * slope_ref[...]).astype(BF16)
    grad = jnp.dot(turned_ref[...], scaled, preferred_element_type=F32).astype(BF16)
    cut = keep_ref.shape[1]
    keep_ref[0] = grad[:cut]
    send_ref[0] = grad[cut:]
    img_out[...] = nt_dot(scaled, w_ref[...]).astype(BF16)


def image_layer(ka, ra, kb, rb, slope, turned, weight):
    pixels, chans = slope.shape
    half = jax.ShapeDtypeStruct((1, chans // 2, chans), BF16)
    return pl.pallas_call(
        image_kernel,
        in_specs=[VMEM] * 7,
        out_specs=[VMEM] * 3,
        out_shape=[jax.ShapeDtypeStruct((pixels, chans), BF16), half, half],
        compiler_params=params(),
        cost_estimate=cost(4 * pixels * chans * chans, 16 * pixels * chans),
        name="image_layer",
    )(ka, ra, kb, rb, slope, turned, weight)


def exchange(value, size_dp, size_tile, flip):
    pairs = []
    for d in range(size_dp):
        for t in range(size_tile):
            dm, tm = flip(t & 1)
            pairs.append((d * size_tile + t, (d ^ dm) * size_tile + (t ^ tm)))
    return lax.ppermute(value, ("dp", "tile"), pairs)


def step_masks(size_dp, size_tile, core):
    dp_masks = [(1 << n, 0) for n in range(int(math.log2(size_dp)))]
    tile_masks = [(0, 1 << n) for n in range(1, int(math.log2(size_tile)))]
    masks = dp_masks + tile_masks
    if core == 1 and len(masks) >= 2:
        masks = [masks[1], masks[0]] + masks[2:]
    return masks


def canonical(masks, size_dp, size_tile):
    dp_bits = int(math.log2(size_dp))
    out = []
    for dm, tm in masks:
        out.append(int(math.log2(dm)) if dm else dp_bits + int(math.log2(tm)) - 1)
    return out


def part_order(me_dp, me_tile, size_dp, size_tile, levels):
    core = me_tile & 1
    dp_bits = int(math.log2(size_dp))
    me = me_dp | ((me_tile >> 1) << dp_bits)
    mine = []
    for which in (0, 1):
        masks = step_masks(size_dp, size_tile, which)[: levels - 1]
        bits = canonical(masks, size_dp, size_tile)
        table = []
        for t in range(1 << (levels - 1)):
            value = 0
            for n, bit in enumerate(bits):
                value |= ((t >> (levels - 2 - n)) & 1) << bit
            table.append(value)
        mine.append(table)
    low_mask = (1 << (levels - 1)) - 1
    tables = jnp.array(mine, jnp.int32)
    same = jnp.where(core == 0, tables[0], tables[1]) ^ (me & low_mask)
    flipped = jnp.where(core == 0, tables[1], tables[0]) ^ (me & low_mask)
    top = 1 << (levels - 1)
    return jnp.concatenate([same + core * top, flipped + (1 - core) * top])


def reduce_parts(keep, send, size_dp, size_tile, levels, scale):
    masks = [step_masks(size_dp, size_tile, core) for core in (0, 1)]
    recv = exchange(send, size_dp, size_tile, lambda core: (0, 1))
    for n in range(levels - 1):
        keep, send = fold(keep, recv)
        recv = exchange(send, size_dp, size_tile, lambda core, n=n: masks[core][n])
    total = keep.astype(F32) + recv.astype(F32)
    for n in range(levels - 1, len(masks[0])):
        value = total.astype(BF16)
        recv = exchange(value, size_dp, size_tile, lambda core, n=n: masks[core][n])
        total = value.astype(F32) + recv.astype(F32)
    return (total * scale).astype(BF16)


def gather_parts(part, size_dp, size_tile, levels):
    masks = [step_masks(size_dp, size_tile, core) for core in (0, 1)]
    for n in reversed(range(levels - 1)):
        recv = exchange(part, size_dp, size_tile, lambda core, n=n: masks[core][n])
        part = jnp.concatenate([part, recv], axis=1)
    recv = exchange(part, size_dp, size_tile, lambda core: (0, 1))
    return part, recv


def place_kernel(parts, shapes, order_ref, *refs):
    count = len(shapes)
    sources = refs[: 2 * count]
    outs = refs[2 * count : 2 * count + 2]
    sem = refs[-1]
    copies = []
    for n, (which, taps) in enumerate(shapes):
        for side in range(2):
            source = sources[2 * n + side]
            size = 2 * source.shape[1] // parts
            for s in range(parts // 2):
                target = pl.multiple_of(order_ref[side * (parts // 2) + s] * size, size)
                for place, tap in enumerate(taps):
                    copies.append(
                        pltpu.make_async_copy(
                            source.at[pl.ds(place * 3, 3), pl.ds(s * size, size)]
                            if which == 0
                            else source.at[0, pl.ds(s * size, size)],
                            outs[0].at[pl.ds(tap * 3, 3), pl.ds(target, size)]
                            if which == 0
                            else outs[1].at[pl.ds(target, size)],
                            sem,
                        )
                    )
    for copy in copies:
        copy.start()
    for copy in copies:
        copy.wait()


def place_parts(order, groups, chans):
    operands = []
    shapes = []
    for which, taps, mine, other in groups:
        operands += [mine, other]
        shapes.append((which, taps))
    return pl.pallas_call(
        functools.partial(place_kernel, order.shape[0], tuple(shapes)),
        in_specs=[SMEM] + [ANY] * len(operands),
        out_specs=[ANY, ANY],
        out_shape=[
            jax.ShapeDtypeStruct((9, chans, chans), BF16),
            jax.ShapeDtypeStruct((chans, chans), BF16),
        ],
        scratch_shapes=[pltpu.SemaphoreType.DMA],
        compiler_params=params(),
        cost_estimate=cost(0, 40 * chans * chans),
        name="place_parts",
    )(order, *operands)


def body(grad_out, bev_act, conv_weight, img_in, backbone_weight, route, offsets, frac_x, frac_y):
    tiles = lax.axis_size("tile")
    pods = lax.axis_size("dp")
    my_tile = lax.axis_index("tile")
    my_pod = lax.axis_index("dp")
    grad = grad_out[0]
    rows, cols, chans = grad.shape
    image = img_in[0]
    weight = jnp.transpose(conv_weight, (1, 2, 0, 3))
    per = image.shape[0] // (2 * IMGW)
    own = rows * cols // BLK
    edge_blocks = cols // BLK
    levels = min(int(math.log2(pods * tiles)), int(math.log2(chans // 16)))
    order = part_order(my_pod, my_tile, pods, tiles, levels)
    cell_scale = 1.0 / math.sqrt(pods * tiles * rows * cols)
    pixel_scale = 1.0 / math.sqrt(pods * tiles * image.shape[0])

    forward = [(i, i + 1) for i in range(tiles - 1)]
    backward = [(b, a) for a, b in forward]
    low = lax.ppermute(grad[rows - 1], "tile", forward)
    high = lax.ppermute(grad[0], "tile", backward)

    core_swap = [(t, t ^ 1) for t in range(tiles)]
    cells = jnp.stack([offsets[0], frac_x[0], frac_y[0]]).reshape(3, own, BLK)
    cells_other = lax.ppermute(cells, "tile", core_swap)
    cells = jnp.concatenate([cells, cells_other], axis=1)
    cells = jnp.concatenate([cells, cells], axis=2)

    inner, edge = bev_inner(grad, weight)
    inner_other = lax.ppermute(inner, "tile", core_swap)
    turned = turn(bev_act[0], order)
    edge = bev_edge(edge, low, high, weight)
    edge_other = lax.ppermute(edge, "tile", core_swap)
    keep_mid, send_mid = wgrad(turned, grad, None, None, (1,))
    as_blocks = lambda value: value.reshape(-1, BLK, chans)
    info = jnp.reshape(my_tile, (1,)).astype(jnp.int32)
    keep_a, send_a, keep_b, send_b = warp_pieces(
        info,
        route[0],
        cells[0],
        cells[1],
        cells[2],
        [as_blocks(v) for v in (inner, edge, inner_other, edge_other)],
        tiles,
        per,
        edge_blocks,
    )
    slope, image_turned = image_slope(order, image, backbone_weight)
    keep_out, send_out = wgrad(turned, grad, low, high, (0, 2))

    tile_masks = [(0, 1 << n) for n in range(1, int(math.log2(tiles)))]
    swapped = [tile_masks[1], tile_masks[0]] + tile_masks[2:] if len(tile_masks) > 1 else tile_masks
    both = (tile_masks, swapped)

    def warp_steps(keep, send):
        for n in range(len(tile_masks)):
            recv = exchange(send, pods, tiles, lambda core, n=n: both[core][n])
            if n == len(tile_masks) - 1:
                return keep.reshape(-1, chans), recv.reshape(-1, chans)
            shape = keep.shape
            keep, send = fold(
                keep.reshape((1, shape[0]) + (shape[1] * shape[2], chans)),
                recv.reshape((1, shape[0]) + (shape[1] * shape[2], chans)),
            )
            keep = keep.reshape((shape[0] // 2,) + shape[1:])
            send = send.reshape((shape[0] // 2,) + shape[1:])

    pair_a = warp_steps(keep_a, send_a)
    pair_b = warp_steps(keep_b, send_b)

    mid = reduce_parts(keep_mid, send_mid, pods, tiles, levels, cell_scale)
    mid = gather_parts(mid, pods, tiles, levels)
    outer = reduce_parts(keep_out, send_out, pods, tiles, levels, cell_scale)
    outer = gather_parts(outer, pods, tiles, levels)

    image_grad, keep_img, send_img = image_layer(*pair_a, *pair_b, slope, image_turned, backbone_weight)
    back = reduce_parts(keep_img, send_img, pods, tiles, levels, pixel_scale)
    back = gather_parts(back, pods, tiles, levels)

    conv_grad, backbone_grad = place_parts(
        order, [(0, (1,)) + mid, (0, (0, 2)) + outer, (1, (0,)) + back], chans
    )
    conv_grad = jnp.transpose(conv_grad.reshape(3, 3, chans, chans), (2, 0, 1, 3))
    return (image_grad[None], conv_grad, backbone_grad)


def solution(mesh):
    return jax.shard_map(
        body,
        mesh=mesh,
        in_specs=(
            P("dp", "tile", None, None),
            P("dp", "tile", None, None),
            P(),
            P("dp", "tile", None),
            P(),
            P("dp", None),
            P("dp", "tile"),
            P("dp", "tile"),
            P("dp", "tile"),
        ),
        out_specs=(P("dp", "tile", None), P(), P()),
        check_vma=False,
    )
```

```python
import functools
import math

import jax
import jax.numpy as jnp
from jax import lax
from jax.experimental import pallas as pl
from jax.experimental.pallas import tpu as pltpu
from jax.sharding import PartitionSpec as P

BLK = 64
IMGW = 64
GROUP = 4
VMEM_BYTES = 56 * 1024 * 1024
F32 = jnp.float32
BF16 = jnp.bfloat16
VMEM = pl.BlockSpec(memory_space=pltpu.VMEM)
SMEM = pl.BlockSpec(memory_space=pltpu.SMEM)
ANY = pl.BlockSpec(memory_space=pl.ANY)


def params(**extra):
    return pltpu.CompilerParams(vmem_limit_bytes=VMEM_BYTES, **extra)


def cost(flops, nbytes):
    return pl.CostEstimate(flops=int(flops), bytes_accessed=int(nbytes), transcendentals=0)


def nt_dot(a, b):
    return lax.dot_general(a, b, (((1,), (1,)), ((), ())), preferred_element_type=F32)


def column_shift(value, by):
    if by == 0:
        return value
    length = value.shape[0]
    place = lax.broadcasted_iota(jnp.int32, value.shape, 0)
    edge = length - 1 if by > 0 else 0
    return jnp.where(place == edge, 0.0, pltpu.roll(value, (-by) % length, 0))


def bev_inner_kernel(g_ref, w_ref, inner_ref, edge_ref, acc_ref):
    rows = g_ref.shape[0]
    step = pl.program_id(0)

    def row_terms(u, taps, j, first):
        lhs = jnp.concatenate([g_ref[u - i + 1] for i in taps], axis=1)
        rhs = jnp.concatenate([w_ref[i, 0] for i in taps], axis=1)
        term = column_shift(nt_dot(lhs, rhs), 1 - j)
        if first:
            acc_ref[u] = term
        else:
            acc_ref[u] = acc_ref[u] + term

    for order, j in enumerate((1, 0, 2)):
        @pl.when(step == order)
        def _(j=j, order=order):
            for u in range(rows):
                taps = (0, 1) if u == 0 else (1, 2) if u == rows - 1 else (0, 1, 2)
                row_terms(u, taps, j, order == 0)

    @pl.when(step == 2)
    def _():
        edge_ref[0] = acc_ref[0]
        edge_ref[1] = acc_ref[rows - 1]

        @pl.loop(1, rows - 1)
        def _(u):
            inner_ref[u - 1] = acc_ref[u].astype(BF16)


def col_tap(step):
    return jnp.where(step == 0, 1, jnp.where(step == 1, 0, 2))


def bev_inner(grad, weight):
    rows, cols, chans = grad.shape
    whole = lambda *shape: pl.BlockSpec(shape, lambda s: (0,) * len(shape))
    return pl.pallas_call(
        bev_inner_kernel,
        grid=(3,),
        in_specs=[
            whole(rows, cols, chans),
            pl.BlockSpec((3, 1, chans, chans), lambda s: (0, col_tap(s), 0, 0)),
        ],
        out_specs=[whole(rows - 2, cols, chans), whole(2, cols, chans)],
        out_shape=[
            jax.ShapeDtypeStruct((rows - 2, cols, chans), BF16),
            jax.ShapeDtypeStruct((2, cols, chans), F32),
        ],
        scratch_shapes=[pltpu.VMEM((rows, cols, chans), F32)],
        compiler_params=params(),
        cost_estimate=cost(2 * (3 * rows - 2) * 3 * cols * chans * chans, 2 * (rows * cols * chans * 2 + 9 * chans * chans)),
        name="bev_inner",
    )(grad, weight)


def bev_edge_kernel(edge_ref, low_ref, high_ref, wl_ref, wh_ref, out_ref, acc_ref):
    step = pl.program_id(0)
    for order, j in enumerate((1, 0, 2)):
        @pl.when(step == order)
        def _(j=j, order=order):
            for side, (halo, w) in enumerate(((low_ref, wl_ref), (high_ref, wh_ref))):
                term = column_shift(nt_dot(halo[...], w[0, 0]), 1 - j)
                base = edge_ref[side] if order == 0 else acc_ref[side]
                if order == 2:
                    out_ref[side] = (base + term).astype(BF16)
                else:
                    acc_ref[side] = base + term


def bev_edge(edge, low, high, weight):
    _, cols, chans = edge.shape
    whole = lambda *shape: pl.BlockSpec(shape, lambda s: (0,) * len(shape))
    return pl.pallas_call(
        bev_edge_kernel,
        grid=(3,),
        in_specs=[
            whole(2, cols, chans),
            whole(cols, chans),
            whole(cols, chans),
            pl.BlockSpec((1, 1, chans, chans), lambda s: (2, col_tap(s), 0, 0)),
            pl.BlockSpec((1, 1, chans, chans), lambda s: (0, col_tap(s), 0, 0)),
        ],
        out_specs=whole(2, cols, chans),
        out_shape=jax.ShapeDtypeStruct((2, cols, chans), BF16),
        scratch_shapes=[pltpu.VMEM((2, cols, chans), F32)],
        compiler_params=params(),
        cost_estimate=cost(2 * 6 * cols * chans * chans, 2 * (8 * cols * chans + 6 * chans * chans)),
        name="bev_edge",
    )(edge, low, high, weight, weight)


def tn_dot(a, b):
    return lax.dot_general(a, b, (((0,), (0,)), ((), ())), preferred_element_type=F32)


def spread(value_ref, order_ref, keep_ref, send_ref):
    parts = order_ref.shape[0]
    size = value_ref.shape[0] // parts
    for half, target in enumerate((keep_ref, send_ref)):
        for s in range(parts // 2):
            source = pl.multiple_of(order_ref[half * (parts // 2) + s] * size, size)
            target[0, s * size : (s + 1) * size, :] = value_ref[pl.ds(source, size), :].astype(BF16)


def wgrad_kernel(taps, halo, order_ref, a_ref, g_ref, *refs):
    if halo:
        low_ref, high_ref = refs[:2]
        refs = refs[2:]
    keep_ref, send_ref, moved_ref, wide_ref = refs[-4:]
    rows, cols, chans = a_ref.shape
    total = rows * cols
    step = pl.program_id(0)
    last = None
    for t, (i, j) in enumerate(taps):
        fresh = j != last
        last = j

        @pl.when(step == t)
        def _(i=i, j=j, fresh=fresh):
            if fresh:
                for u in range(rows):
                    if j == 1:
                        moved_ref[u * cols : (u + 1) * cols, :] = a_ref[u]
                    else:
                        moved_ref[u * cols : (u + 1) * cols, :] = column_shift(
                            a_ref[u].astype(F32), j - 1
                        ).astype(BF16)
            if i == 1:
                wide_ref[...] = tn_dot(moved_ref[...], g_ref[...])
            elif i == 0:
                wide_ref[...] = tn_dot(moved_ref[: total - cols, :], g_ref[cols:, :]) + tn_dot(
                    moved_ref[total - cols :, :], high_ref[...]
                )
            else:
                wide_ref[...] = tn_dot(moved_ref[cols:, :], g_ref[: total - cols, :]) + tn_dot(
                    moved_ref[:cols, :], low_ref[...]
                )
            spread(wide_ref, order_ref, keep_ref, send_ref)


def wgrad(order, act, grad, halos, after, taps):
    rows, cols, chans = grad.shape
    count = len(taps)
    whole = lambda *shape: pl.BlockSpec(shape, lambda t: (0,) * len(shape))
    half_spec = pl.BlockSpec((1, chans // 2, chans), lambda t: (t, 0, 0))
    shape = jax.ShapeDtypeStruct((count, chans // 2, chans), BF16)
    return pl.pallas_call(
        functools.partial(wgrad_kernel, taps, len(halos) > 0),
        grid=(count,),
        in_specs=[SMEM, whole(rows, cols, chans), whole(rows * cols, chans)]
        + [whole(cols, chans)] * len(halos)
        + [ANY] * len(after),
        out_specs=[half_spec, half_spec],
        out_shape=[shape, shape],
        scratch_shapes=[pltpu.VMEM((rows * cols, chans), BF16), pltpu.VMEM((chans, chans), F32)],
        compiler_params=params(),
        cost_estimate=cost(
            2 * count * rows * cols * chans * chans, 2 * (2 * rows * cols * chans + count * chans * chans)
        ),
        name="wgrad",
    )(order, act, grad.reshape(rows * cols, chans), *halos, *after)


def pieces_kernel(
    plan, info_ref, route_ref, off_ref, fx_ref, fy_ref, *refs
):
    own_blocks, per, tile_bits, edge = plan
    sources = refs[:4]
    outs = refs[4:8]
    blocks_ref, acc_ref, count_ref, list_ref, sems = refs[8:]
    copies = []
    start = 0
    for n, source in enumerate(sources):
        size = source.shape[0]
        copies.append(pltpu.make_async_copy(source, blocks_ref.at[pl.ds(start, size)], sems.at[n]))
        start += size
    for copy in copies:
        copy.start()
    tile = info_ref[0]
    core = tile & 1
    slots = outs[0].shape[0] * 2
    half_per = outs[0].shape[1]
    wide = 2 * own_blocks
    inner = own_blocks - 2 * edge

    @pl.loop(0, slots * per)
    def _(n):
        count_ref[n] = 0

    @pl.loop(0, wide)
    def _(n):
        other = n // own_blocks
        k = n - other * own_blocks
        ident = route_ref[(tile ^ other) * own_blocks + k]
        owner = ident // per
        local = ident - owner * per
        away = (owner ^ tile) >> 1

        @pl.when(((owner ^ tile) & 1) == 0)
        def _():
            place = slot_of(away, core, tile_bits)
            at = place * per + local
            have = count_ref[at]
            list_ref[at * wide + have] = n
            count_ref[at] = have + 1

    for copy in copies:
        copy.wait()

    lanes = lax.broadcasted_iota(jnp.int32, (1, 2 * BLK), 1)
    low_lane = lanes < BLK

    def group_product(at, first, have):
        picked = []
        for g in range(GROUP):
            there = first + g < have
            n = jnp.where(there, list_ref[at * wide + jnp.minimum(first + g, wide - 1)], 0)
            other = n // own_blocks
            k = n - other * own_blocks
            spot = jnp.where(
                k < edge, inner + k, jnp.where(k >= own_blocks - edge, inner + k - inner, k - edge)
            )
            picked.append((there, n, other * own_blocks + spot))
        rhs = jnp.concatenate([blocks_ref[spot] for _, _, spot in picked], axis=0)

        def lane_row(ref):
            halves = []
            for p in range(0, GROUP, 2):
                a = ref[pl.ds(picked[p][1], 1), :]
                b = ref[pl.ds(picked[p + 1][1], 1), :]
                halves.append(jnp.where(low_lane, a, b))
            return jnp.concatenate(halves, axis=1)

        valid = jnp.concatenate(
            [
                jnp.where(
                    low_lane,
                    jnp.where(picked[p][0], 1.0, 0.0),
                    jnp.where(picked[p + 1][0], 1.0, 0.0),
                )
                for p in range(0, GROUP, 2)
            ],
            axis=1,
        ).astype(F32)
        left = lane_row(off_ref)
        right_w = lane_row(fx_ref).astype(F32) / 256.0
        lower_w = lane_row(fy_ref).astype(F32) / 256.0
        column = lax.broadcasted_iota(jnp.int32, (IMGW, GROUP * BLK), 0)
        across = jnp.where(column == left, 1.0 - right_w, 0.0) + jnp.where(
            column == left + 1, right_w, 0.0
        )
        band = jnp.concatenate(
            [((1.0 - lower_w) * valid) * across, (lower_w * valid) * across], axis=0
        ).astype(BF16)
        return jnp.dot(band, rhs, preferred_element_type=F32)

    def fill(out, place, local, inside):
        at = place * per + local
        have = count_ref[at]
        out[inside[0], inside[1]] = group_product(at, 0, have).astype(BF16)

    def overfill(out, place, local, inside):
        at = place * per + local
        have = count_ref[at]

        @pl.when(have > GROUP)
        def _():
            acc_ref[...] = jnp.zeros_like(acc_ref)

            @pl.loop(0, (have + GROUP - 1) // GROUP)
            def _(m):
                acc_ref[...] = acc_ref[...] + group_product(at, m * GROUP, have)

            out[inside[0], inside[1]] = acc_ref[...].astype(BF16)

    for chunk in range(2):
        for half in (1, 0):
            out = outs[2 * chunk + half]

            def visit(n, step, out=out, half=half, chunk=chunk):
                place = n // half_per
                local = n - place * half_per
                step(out, half * (slots // 2) + place, chunk * half_per + local, (place, local))

            pl.loop(0, (slots // 2) * half_per, unroll=4)(functools.partial(visit, step=fill))
            pl.loop(0, (slots // 2) * half_per)(functools.partial(visit, step=overfill))


def swap_low_bits(value):
    return (value & ~3) | ((value & 1) << 1) | ((value >> 1) & 1)


def slot_of(away, core, bits):
    place = 0
    first = jnp.where((core == 1) & (bits >= 2), swap_low_bits(away), away)
    for n in range(bits):
        place = place | (((first >> n) & 1) << (bits - 1 - n))
    return place


def warp_pieces(info, route, off, fx, fy, sources, tiles, per, edge):
    own = sources[0].shape[0] + sources[1].shape[0]
    chans = sources[0].shape[2]
    bits = int(math.log2(tiles)) - 1
    slots = tiles // 2
    shape = jax.ShapeDtypeStruct((slots // 2, per // 2, 2 * IMGW, chans), BF16)
    return pl.pallas_call(
        functools.partial(pieces_kernel, (own, per, bits, edge)),
        in_specs=[SMEM, SMEM, VMEM, VMEM, VMEM] + [ANY] * 4,
        out_specs=[VMEM] * 4,
        out_shape=[shape] * 4,
        scratch_shapes=[
            pltpu.VMEM((2 * own, BLK, chans), BF16),
            pltpu.VMEM((2 * IMGW, chans), F32),
            pltpu.SMEM((slots * per,), jnp.int32),
            pltpu.SMEM((slots * per * 2 * own,), jnp.int32),
            pltpu.SemaphoreType.DMA((4,)),
        ],
        compiler_params=params(),
        cost_estimate=cost(
            2 * slots * per * 2 * IMGW * GROUP * BLK * chans, 2 * (own * 2 * BLK * chans + slots * per * 2 * IMGW * chans)
        ),
        name="warp_pieces",
    )(info, route, off, fx, fy, *sources)


def slope_kernel(img_ref, w_ref, slope_ref):
    value = jnp.dot(img_ref[...], w_ref[...], preferred_element_type=F32)
    sigma = jax.nn.sigmoid(value)
    slope_ref[...] = sigma * (1.0 + value * (1.0 - sigma))


def image_slope(image, weight):
    pixels, chans = image.shape
    return pl.pallas_call(
        slope_kernel,
        in_specs=[VMEM, VMEM],
        out_specs=VMEM,
        out_shape=jax.ShapeDtypeStruct((pixels, chans), F32),
        compiler_params=params(),
        cost_estimate=cost(2 * pixels * chans * chans, 10 * pixels * chans),
        name="image_slope",
    )(image, weight)


def image_kernel(chunks, order_ref, *refs):
    terms = refs[: sum(chunks)]
    slope_ref, image_ref, w_ref, img_out, keep_ref, send_ref, wide_ref = refs[sum(chunks) :]
    feature = []
    start = 0
    for size in chunks:
        total = terms[start][0].astype(F32)
        for term in terms[start + 1 : start + size]:
            total = total + term[0].astype(F32)
        feature.append(total.reshape(-1, total.shape[-1]))
        start += size
    feature = jnp.concatenate(feature, axis=0)
    scaled = (feature * slope_ref[...]).astype(BF16)
    wide_ref[...] = tn_dot(image_ref[...], scaled)
    spread(wide_ref, order_ref, keep_ref, send_ref)
    img_out[...] = nt_dot(scaled, w_ref[...]).astype(BF16)


def image_layer(order, chunks, slope, image, weight):
    pixels, chans = slope.shape
    half = jax.ShapeDtypeStruct((1, chans // 2, chans), BF16)
    whole = lambda *shape: pl.BlockSpec(shape, lambda n: (0,) * len(shape))
    terms = [term for chunk in chunks for term in chunk]
    return pl.pallas_call(
        functools.partial(image_kernel, tuple(len(chunk) for chunk in chunks)),
        grid=(1,),
        in_specs=[SMEM]
        + [whole(1, *term.shape[1:]) for term in terms]
        + [whole(pixels, chans), whole(pixels, chans), whole(chans, chans)],
        out_specs=[whole(pixels, chans), whole(1, chans // 2, chans), whole(1, chans // 2, chans)],
        out_shape=[jax.ShapeDtypeStruct((pixels, chans), BF16), half, half],
        scratch_shapes=[pltpu.VMEM((chans, chans), F32)],
        compiler_params=params(),
        cost_estimate=cost(4 * pixels * chans * chans, 16 * pixels * chans),
        name="image_layer",
    )(order, *terms, slope, image, weight)


def exchange(value, size_dp, size_tile, flip):
    pairs = []
    for d in range(size_dp):
        for t in range(size_tile):
            dm, tm = flip(t & 1)
            pairs.append((d * size_tile + t, (d ^ dm) * size_tile + (t ^ tm)))
    return lax.ppermute(value, ("dp", "tile"), pairs)


def step_masks(size_dp, size_tile, core):
    dp_masks = [(1 << n, 0) for n in range(int(math.log2(size_dp)))]
    tile_masks = [(0, 1 << n) for n in range(1, int(math.log2(size_tile)))]
    masks = dp_masks + tile_masks
    if core == 1 and len(masks) >= 2:
        masks = [masks[1], masks[0]] + masks[2:]
    return masks


def canonical(masks, size_dp, size_tile):
    dp_bits = int(math.log2(size_dp))
    out = []
    for dm, tm in masks:
        out.append(int(math.log2(dm)) if dm else dp_bits + int(math.log2(tm)) - 1)
    return out


def part_order(me_dp, me_tile, size_dp, size_tile, levels):
    core = me_tile & 1
    dp_bits = int(math.log2(size_dp))
    me = me_dp | ((me_tile >> 1) << dp_bits)
    mine = []
    for which in (0, 1):
        masks = step_masks(size_dp, size_tile, which)[: levels - 1]
        bits = canonical(masks, size_dp, size_tile)
        table = []
        for t in range(1 << (levels - 1)):
            value = 0
            for n, bit in enumerate(bits):
                value |= ((t >> (levels - 2 - n)) & 1) << bit
            table.append(value)
        mine.append(table)
    low_mask = (1 << (levels - 1)) - 1
    tables = jnp.array(mine, jnp.int32)
    same = jnp.where(core == 0, tables[0], tables[1]) ^ (me & low_mask)
    flipped = jnp.where(core == 0, tables[1], tables[0]) ^ (me & low_mask)
    top = 1 << (levels - 1)
    return jnp.concatenate([same + core * top, flipped + (1 - core) * top])


def region_sum(terms, axis, low, high):
    total = lax.slice_in_dim(terms[0], low, high, axis=axis).astype(F32)
    for term in terms[1:]:
        total = total + lax.slice_in_dim(term, low, high, axis=axis).astype(F32)
    return total


def reduce_parts(keep, send, size_dp, size_tile, levels, scale):
    masks = [step_masks(size_dp, size_tile, core) for core in (0, 1)]
    terms = [keep, exchange(send, size_dp, size_tile, lambda core: (0, 1))]
    extent = keep.shape[1]
    for n in range(levels - 1):
        send = region_sum(terms, 1, extent // 2, extent).astype(BF16)
        extent //= 2
        terms.append(exchange(send, size_dp, size_tile, lambda core, n=n: masks[core][n]))
    total = region_sum(terms, 1, 0, extent)
    for n in range(levels - 1, len(masks[0])):
        value = total.astype(BF16)
        recv = exchange(value, size_dp, size_tile, lambda core, n=n: masks[core][n])
        total = value.astype(F32) + recv.astype(F32)
    return (total * scale).astype(BF16)


def gather_parts(part, size_dp, size_tile, levels):
    masks = [step_masks(size_dp, size_tile, core) for core in (0, 1)]
    for n in reversed(range(levels - 1)):
        recv = exchange(part, size_dp, size_tile, lambda core, n=n: masks[core][n])
        part = jnp.concatenate([part, recv], axis=1)
    recv = exchange(part, size_dp, size_tile, lambda core: (0, 1))
    return part, recv


def warp_steps(keep, send, size_dp, size_tile):
    tile_masks = [(0, 1 << n) for n in range(1, int(math.log2(size_tile)))]
    swapped = [tile_masks[1], tile_masks[0]] + tile_masks[2:] if len(tile_masks) > 1 else tile_masks
    both = (tile_masks, swapped)
    terms = [keep]
    extent = keep.shape[0]
    for n in range(len(tile_masks)):
        if n > 0:
            send = region_sum(terms, 0, extent // 2, extent).astype(BF16)
            extent //= 2
        terms.append(exchange(send, size_dp, size_tile, lambda core, n=n: both[core][n]))
    return terms


def place_kernel(order_ref, mine_ref, other_ref, *refs):
    out_ref = refs[-1]
    parts = order_ref.shape[0]
    size = out_ref.shape[1] // parts
    for half, source in enumerate((mine_ref, other_ref)):
        for s in range(parts // 2):
            target = pl.multiple_of(order_ref[half * (parts // 2) + s] * size, size)
            out_ref[0, pl.ds(target, size), :] = source[0, s * size : (s + 1) * size, :]


def place_parts(order, mine, other, places, count, before):
    chans = mine.shape[2]

    def target(t):
        place = places[0]
        for n, value in enumerate(places):
            place = jnp.where(t == n, value, place)
        return (place, 0, 0)

    half_spec = pl.BlockSpec((1, chans // 2, chans), lambda t: (t, 0, 0))
    return pl.pallas_call(
        place_kernel,
        grid=(len(places),),
        in_specs=[SMEM, half_spec, half_spec] + [ANY] * len(before),
        out_specs=pl.BlockSpec((1, chans, chans), target),
        out_shape=jax.ShapeDtypeStruct((count, chans, chans), BF16),
        input_output_aliases={3: 0} if before else {},
        compiler_params=params(),
        cost_estimate=cost(0, 4 * len(places) * chans * chans),
        name="place_parts",
    )(order, mine, other, *before)


def body(grad_out, bev_act, conv_weight, img_in, backbone_weight, route, offsets, frac_x, frac_y):
    tiles = lax.axis_size("tile")
    pods = lax.axis_size("dp")
    my_tile = lax.axis_index("tile")
    my_pod = lax.axis_index("dp")
    grad = grad_out[0]
    rows, cols, chans = grad.shape
    image = img_in[0]
    weight = jnp.transpose(conv_weight, (1, 2, 0, 3))
    per = image.shape[0] // (2 * IMGW)
    own = rows * cols // BLK
    edge_blocks = cols // BLK
    levels = min(int(math.log2(pods * tiles)), int(math.log2(chans // 16)))
    order = part_order(my_pod, my_tile, pods, tiles, levels)
    cell_scale = 1.0 / math.sqrt(pods * tiles * rows * cols)
    pixel_scale = 1.0 / math.sqrt(pods * tiles * image.shape[0])

    forward = [(i, i + 1) for i in range(tiles - 1)]
    backward = [(b, a) for a, b in forward]
    low = lax.ppermute(grad[rows - 1], "tile", forward)
    high = lax.ppermute(grad[0], "tile", backward)

    core_swap = [(t, t ^ 1) for t in range(tiles)]
    cells = jnp.stack([offsets[0], frac_x[0], frac_y[0]]).reshape(3, own, BLK)
    cells_other = lax.ppermute(cells, "tile", core_swap)
    cells = jnp.concatenate([cells, cells_other], axis=1)
    cells = jnp.concatenate([cells, cells], axis=2)

    inner, edge = bev_inner(grad, weight)
    inner_other = lax.ppermute(inner, "tile", core_swap)
    mid_taps = ((1, 1), (1, 0), (1, 2))
    outer_taps = ((0, 1), (2, 1), (0, 0), (2, 0), (0, 2), (2, 2))
    keep_mid, send_mid = wgrad(order, bev_act[0], grad, [], [inner], mid_taps)
    edge = bev_edge(edge, low, high, weight)
    edge_other = lax.ppermute(edge, "tile", core_swap)
    slope = image_slope(image, backbone_weight)
    as_blocks = lambda value: value.reshape(-1, BLK, chans)
    info = jnp.reshape(my_tile, (1,)).astype(jnp.int32)
    keep_a, send_a, keep_b, send_b = warp_pieces(
        info,
        route[0],
        cells[0],
        cells[1],
        cells[2],
        [as_blocks(v) for v in (inner, edge, inner_other, edge_other)],
        tiles,
        per,
        edge_blocks,
    )
    keep_out, send_out = wgrad(order, bev_act[0], grad, [low, high], [keep_a], outer_taps)
    chunk_a = warp_steps(keep_a, send_a, pods, tiles)
    chunk_b = warp_steps(keep_b, send_b, pods, tiles)

    mid = reduce_parts(keep_mid, send_mid, pods, tiles, levels, cell_scale)
    mid = gather_parts(mid, pods, tiles, levels)
    outer = reduce_parts(keep_out, send_out, pods, tiles, levels, cell_scale)
    outer = gather_parts(outer, pods, tiles, levels)

    image_grad, keep_img, send_img = image_layer(
        order, [chunk_a, chunk_b], slope, image, backbone_weight
    )
    back = reduce_parts(keep_img, send_img, pods, tiles, levels, pixel_scale)
    back = gather_parts(back, pods, tiles, levels)

    tap_place = lambda taps: [3 * i + j for i, j in taps]
    conv_grad = place_parts(order, *mid, tap_place(mid_taps), 9, [])
    conv_grad = place_parts(order, *outer, tap_place(outer_taps), 9, [conv_grad])
    backbone_grad = place_parts(order, *back, [0], 1, [])[0]
    conv_grad = jnp.transpose(conv_grad.reshape(3, 3, chans, chans), (2, 0, 1, 3))
    return (image_grad[None], conv_grad, backbone_grad)


def solution(mesh):
    return jax.shard_map(
        body,
        mesh=mesh,
        in_specs=(
            P("dp", "tile", None, None),
            P("dp", "tile", None, None),
            P(),
            P("dp", "tile", None),
            P(),
            P("dp", None),
            P("dp", "tile"),
            P("dp", "tile"),
            P("dp", "tile"),
        ),
        out_specs=(P("dp", "tile", None), P(), P()),
        check_vma=False,
    )
```

```python
import functools
import math

import jax
import jax.numpy as jnp
from jax import lax
from jax.experimental import pallas as pl
from jax.experimental.pallas import tpu as pltpu
from jax.sharding import PartitionSpec as P

BLK = 64
IMGW = 64
GROUP = 4
BATCH = 4
CONV_LEVELS = 3
VMEM_BYTES = 63 * 1024 * 1024
F32 = jnp.float32
BF16 = jnp.bfloat16
VMEM = pl.BlockSpec(memory_space=pltpu.VMEM)
SMEM = pl.BlockSpec(memory_space=pltpu.SMEM)
ANY = pl.BlockSpec(memory_space=pl.ANY)


def params(**extra):
    return pltpu.CompilerParams(vmem_limit_bytes=VMEM_BYTES, **extra)


def cost(flops, nbytes):
    return pl.CostEstimate(flops=int(flops), bytes_accessed=int(nbytes), transcendentals=0)


def nt_dot(a, b):
    return lax.dot_general(a, b, (((1,), (1,)), ((), ())), preferred_element_type=F32)


def column_shift(value, by):
    if by == 0:
        return value
    length = value.shape[0]
    place = lax.broadcasted_iota(jnp.int32, value.shape, 0)
    edge = length - 1 if by > 0 else 0
    return jnp.where(place == edge, 0.0, pltpu.roll(value, (-by) % length, 0))


def bev_kernel(targets, halo, g_ref, *refs):
    if halo:
        low_ref, high_ref = refs[:2]
        refs = refs[2:]
    w_ref, out_ref, acc_ref = refs
    rows = g_ref.shape[0]
    step = pl.program_id(0)

    def frame(u):
        if u < 0:
            return low_ref[...]
        if u >= rows:
            return high_ref[...]
        return g_ref[u]

    for order, j in enumerate((1, 0, 2)):
        @pl.when(step == order)
        def _(j=j, order=order):
            rhs = jnp.concatenate([w_ref[i, 0] for i in range(3)], axis=1)
            for n, u in enumerate(targets):
                lhs = jnp.concatenate([frame(u - i + 1) for i in range(3)], axis=1)
                term = column_shift(nt_dot(lhs, rhs), 1 - j)
                if order == 0:
                    acc_ref[n] = term
                elif order == 1:
                    acc_ref[n] = acc_ref[n] + term
                else:
                    out_ref[n] = (acc_ref[n] + term).astype(BF16)


def col_tap(step):
    return jnp.where(step == 0, 1, jnp.where(step == 1, 0, 2))


def bev_rows(grad, halos, weight, targets, after):
    rows, cols, chans = grad.shape
    whole = lambda *shape: pl.BlockSpec(shape, lambda s: (0,) * len(shape))
    count = len(targets)

    def kernel(g_ref, *refs):
        n = len(halos) + 1
        bev_kernel(targets, len(halos) > 0, g_ref, *refs[:n], *refs[n + len(after) :])

    return pl.pallas_call(
        kernel,
        grid=(3,),
        in_specs=[whole(rows, cols, chans)]
        + [whole(cols, chans)] * len(halos)
        + [pl.BlockSpec((3, 1, chans, chans), lambda s: (0, col_tap(s), 0, 0))]
        + [ANY] * len(after),
        out_specs=whole(count, cols, chans),
        out_shape=jax.ShapeDtypeStruct((count, cols, chans), BF16),
        scratch_shapes=[pltpu.VMEM((count, cols, chans), F32)],
        compiler_params=params(),
        cost_estimate=cost(18 * count * cols * chans * chans, 2 * (2 * rows * cols * chans + 9 * chans * chans)),
        name="bev_rows",
    )(grad, *halos, weight, *after)


def tn_dot(a, b):
    return lax.dot_general(a, b, (((0,), (0,)), ((), ())), preferred_element_type=F32)


def spread(value_ref, order_ref, keep_ref, send_ref):
    parts = order_ref.shape[0]
    size = value_ref.shape[0] // parts
    for half, target in enumerate((keep_ref, send_ref)):
        for s in range(parts // 2):
            source = pl.multiple_of(order_ref[half * (parts // 2) + s] * size, size)
            target[0, s * size : (s + 1) * size, :] = value_ref[pl.ds(source, size), :].astype(BF16)


def wgrad_kernel(taps, halo, order_ref, a_ref, g_ref, *refs):
    if halo:
        low_ref, high_ref = refs[:2]
    keep_ref, send_ref, moved_ref, wide_ref = refs[-4:]
    rows, cols, chans = a_ref.shape
    total = rows * cols
    step = pl.program_id(0)
    for t, (i, j) in enumerate(taps):
        fresh = j != 1 and (t == 0 or taps[t - 1][1] != j)

        @pl.when(step == t)
        def _(i=i, j=j, fresh=fresh):
            if fresh:
                for u in range(rows):
                    moved_ref[u * cols : (u + 1) * cols, :] = column_shift(
                        a_ref[u].astype(F32), j - 1
                    ).astype(BF16)
            if j == 1:
                act = lambda low, high: a_ref[low:high].reshape((high - low) * cols, chans)
            else:
                act = lambda low, high: moved_ref[low * cols : high * cols, :]
            if i == 1:
                wide_ref[...] = tn_dot(act(0, rows), g_ref[...])
            elif i == 0:
                wide_ref[...] = tn_dot(act(0, rows - 1), g_ref[cols:, :]) + tn_dot(
                    act(rows - 1, rows), high_ref[...]
                )
            else:
                wide_ref[...] = tn_dot(act(1, rows), g_ref[: total - cols, :]) + tn_dot(
                    act(0, 1), low_ref[...]
                )
            spread(wide_ref, order_ref, keep_ref, send_ref)


def pick(index, values):
    result = values[0]
    for n, value in enumerate(values):
        result = jnp.where(index == n, value, result)
    return result


def wgrad(order, act, grad, halos, taps, places, count, before, after):
    rows, cols, chans = grad.shape
    whole = lambda *shape: pl.BlockSpec(shape, lambda t: (0,) * len(shape))
    half_spec = pl.BlockSpec((1, chans // 2, chans), lambda t: (pick(t, places), 0, 0))
    shape = jax.ShapeDtypeStruct((count, chans // 2, chans), BF16)
    ahead = 3 + len(halos)
    return pl.pallas_call(
        functools.partial(wgrad_kernel, taps, len(halos) > 0),
        grid=(len(taps),),
        in_specs=[SMEM, whole(rows, cols, chans), whole(rows * cols, chans)]
        + [whole(cols, chans)] * len(halos)
        + [ANY] * (len(before) + len(after)),
        out_specs=[half_spec, half_spec],
        out_shape=[shape, shape],
        scratch_shapes=[pltpu.VMEM((rows * cols, chans), BF16), pltpu.VMEM((chans, chans), F32)],
        input_output_aliases={ahead: 0, ahead + 1: 1} if before else {},
        compiler_params=params(),
        cost_estimate=cost(
            2 * len(taps) * rows * cols * chans * chans,
            2 * (2 * rows * cols * chans + len(taps) * chans * chans),
        ),
        name="wgrad",
    )(order, act, grad.reshape(rows * cols, chans), *halos, *before, *after)


def pieces_kernel(
    plan, info_ref, route_ref, mine_ref, other_ref, *refs
):
    own_blocks, per, tile_bits, edge, after = plan
    sources = refs[:4]
    outs = refs[4 + after : 6 + after]
    blocks_ref, cells_ref, acc_ref, count_ref, list_ref, sems = refs[6 + after :]
    off_ref, fx_ref, fy_ref = cells_ref.at[0], cells_ref.at[1], cells_ref.at[2]
    copies = []
    start = 0
    for n, source in enumerate(sources):
        size = source.shape[0]
        copies.append(pltpu.make_async_copy(source, blocks_ref.at[pl.ds(start, size)], sems.at[n]))
        start += size
    for copy in copies:
        copy.start()
    for n in range(3):
        for start, cells in ((0, mine_ref), (own_blocks, other_ref)):
            cells_ref[n, start : start + own_blocks, :] = jnp.concatenate([cells[n], cells[n]], axis=1)
    tile = info_ref[0]
    core = tile & 1
    slots = outs[0].shape[0] * 2
    wide = 2 * own_blocks
    inner = own_blocks - 2 * edge

    @pl.loop(0, slots * per)
    def _(n):
        count_ref[n] = 0

    @pl.loop(0, wide)
    def _(n):
        other = n // own_blocks
        k = n - other * own_blocks
        ident = route_ref[(tile ^ other) * own_blocks + k]
        owner = ident // per
        local = ident - owner * per
        away = (owner ^ tile) >> 1

        @pl.when(((owner ^ tile) & 1) == 0)
        def _():
            place = slot_of(away, core, tile_bits)
            at = place * per + local
            have = count_ref[at]
            list_ref[at * wide + have] = n
            count_ref[at] = have + 1

    for copy in copies:
        copy.wait()

    lanes = lax.broadcasted_iota(jnp.int32, (1, 2 * BLK), 1)
    low_lane = lanes < BLK

    def group_product(at, first, have):
        picked = []
        for g in range(GROUP):
            there = first + g < have
            n = jnp.where(there, list_ref[at * wide + jnp.minimum(first + g, wide - 1)], 0)
            other = n // own_blocks
            k = n - other * own_blocks
            spot = jnp.where(
                k < edge, inner + k, jnp.where(k >= own_blocks - edge, inner + k - inner, k - edge)
            )
            picked.append((there, n, other * own_blocks + spot))
        rhs = jnp.concatenate([blocks_ref[spot] for _, _, spot in picked], axis=0)

        def lane_row(ref):
            halves = []
            for p in range(0, GROUP, 2):
                a = ref[pl.ds(picked[p][1], 1), :]
                b = ref[pl.ds(picked[p + 1][1], 1), :]
                halves.append(jnp.where(low_lane, a, b))
            return jnp.concatenate(halves, axis=1)

        valid = jnp.concatenate(
            [
                jnp.where(
                    low_lane,
                    jnp.where(picked[p][0], 1.0, 0.0),
                    jnp.where(picked[p + 1][0], 1.0, 0.0),
                )
                for p in range(0, GROUP, 2)
            ],
            axis=1,
        ).astype(F32)
        left = lane_row(off_ref)
        right_w = lane_row(fx_ref).astype(F32) / 256.0
        lower_w = lane_row(fy_ref).astype(F32) / 256.0
        column = lax.broadcasted_iota(jnp.int32, (IMGW, GROUP * BLK), 0)
        across = jnp.where(column == left, 1.0 - right_w, 0.0) + jnp.where(
            column == left + 1, right_w, 0.0
        )
        band = jnp.concatenate(
            [((1.0 - lower_w) * valid) * across, (lower_w * valid) * across], axis=0
        ).astype(BF16)
        return jnp.dot(band, rhs, preferred_element_type=F32)

    def overfill(out, place, local, inside):
        at = place * per + local
        have = count_ref[at]

        @pl.when(have > GROUP)
        def _():
            acc_ref[...] = jnp.zeros_like(acc_ref)

            @pl.loop(0, (have + GROUP - 1) // GROUP)
            def _(m):
                acc_ref[...] = acc_ref[...] + group_product(at, m * GROUP, have)

            out[inside[0], inside[1]] = acc_ref[...].astype(BF16)

    for half in (1, 0):
        out = outs[half]
        base = half * (slots // 2)

        @pl.loop(0, (slots // 2) * per // BATCH)
        def _(m, out=out, base=base):
            values = []
            for n in range(BATCH):
                at = base * per + m * BATCH + n
                values.append(group_product(at, 0, count_ref[at]).astype(BF16))
            for n in range(BATCH):
                spot = m * BATCH + n
                out[spot // per, spot % per] = values[n]

        @pl.loop(0, (slots // 2) * per)
        def _(spot, out=out, base=base):
            overfill(out, base + spot // per, spot % per, (spot // per, spot % per))


def swap_low_bits(value):
    return (value & ~3) | ((value & 1) << 1) | ((value >> 1) & 1)


def slot_of(away, core, bits):
    place = 0
    first = jnp.where((core == 1) & (bits >= 2), swap_low_bits(away), away)
    for n in range(bits):
        place = place | (((first >> n) & 1) << (bits - 1 - n))
    return place


def warp_pieces(info, route, cells, cells_other, sources, tiles, per, edge, after):
    own = sources[0].shape[0] + sources[1].shape[0]
    chans = sources[0].shape[2]
    bits = int(math.log2(tiles)) - 1
    slots = tiles // 2
    shape = jax.ShapeDtypeStruct((slots // 2, per, 2 * IMGW, chans), BF16)
    return pl.pallas_call(
        functools.partial(pieces_kernel, (own, per, bits, edge, len(after))),
        in_specs=[SMEM, SMEM, VMEM, VMEM] + [ANY] * (4 + len(after)),
        out_specs=[VMEM] * 2,
        out_shape=[shape] * 2,
        scratch_shapes=[
            pltpu.VMEM((2 * own, BLK, chans), BF16),
            pltpu.VMEM((3, 2 * own, 2 * BLK), jnp.int32),
            pltpu.VMEM((2 * IMGW, chans), F32),
            pltpu.SMEM((slots * per,), jnp.int32),
            pltpu.SMEM((slots * per * 2 * own,), jnp.int32),
            pltpu.SemaphoreType.DMA((4,)),
        ],
        compiler_params=params(),
        cost_estimate=cost(
            2 * slots * per * 2 * IMGW * GROUP * BLK * chans, 2 * (own * 2 * BLK * chans + slots * per * 2 * IMGW * chans)
        ),
        name="warp_pieces",
    )(info, route, cells, cells_other, *sources, *after)


def slope_kernel(img_ref, w_ref, *refs):
    slope_ref = refs[-1]
    value = jnp.dot(img_ref[...], w_ref[...], preferred_element_type=F32)
    sigma = jax.nn.sigmoid(value)
    slope_ref[...] = sigma * (1.0 + value * (1.0 - sigma))


def image_slope(image, weight, after):
    pixels, chans = image.shape
    return pl.pallas_call(
        slope_kernel,
        in_specs=[VMEM, VMEM] + [ANY] * len(after),
        out_specs=VMEM,
        out_shape=jax.ShapeDtypeStruct((pixels, chans), F32),
        compiler_params=params(),
        cost_estimate=cost(2 * pixels * chans * chans, 10 * pixels * chans),
        name="image_slope",
    )(image, weight, *after)


def image_kernel(chunks, order_ref, *refs):
    terms = refs[: sum(chunks)]
    slope_ref, image_ref, w_ref, img_out, keep_ref, send_ref, wide_ref = refs[sum(chunks) :]
    feature = []
    start = 0
    for size in chunks:
        total = terms[start][0].astype(F32)
        for term in terms[start + 1 : start + size]:
            total = total + term[0].astype(F32)
        feature.append(total.reshape(-1, total.shape[-1]))
        start += size
    feature = jnp.concatenate(feature, axis=0)
    scaled = (feature * slope_ref[...]).astype(BF16)
    wide_ref[...] = tn_dot(image_ref[...], scaled)
    spread(wide_ref, order_ref, keep_ref, send_ref)
    img_out[...] = nt_dot(scaled, w_ref[...]).astype(BF16)


def image_layer(order, chunks, slope, image, weight):
    pixels, chans = slope.shape
    half = jax.ShapeDtypeStruct((1, chans // 2, chans), BF16)
    whole = lambda *shape: pl.BlockSpec(shape, lambda n: (0,) * len(shape))
    terms = [term for chunk in chunks for term in chunk]
    return pl.pallas_call(
        functools.partial(image_kernel, tuple(len(chunk) for chunk in chunks)),
        grid=(1,),
        in_specs=[SMEM]
        + [whole(1, *term.shape[1:]) for term in terms]
        + [whole(pixels, chans), whole(pixels, chans), whole(chans, chans)],
        out_specs=[whole(pixels, chans), whole(1, chans // 2, chans), whole(1, chans // 2, chans)],
        out_shape=[jax.ShapeDtypeStruct((pixels, chans), BF16), half, half],
        scratch_shapes=[pltpu.VMEM((chans, chans), F32)],
        compiler_params=params(),
        cost_estimate=cost(4 * pixels * chans * chans, 16 * pixels * chans),
        name="image_layer",
    )(order, *terms, slope, image, weight)


def exchange(value, size_dp, size_tile, flip):
    pairs = []
    for d in range(size_dp):
        for t in range(size_tile):
            dm, tm = flip(t & 1)
            pairs.append((d * size_tile + t, (d ^ dm) * size_tile + (t ^ tm)))
    return lax.ppermute(value, ("dp", "tile"), pairs)


def step_masks(size_dp, size_tile, core):
    dp_masks = [(1 << n, 0) for n in range(int(math.log2(size_dp)))]
    tile_masks = [(0, 1 << n) for n in range(1, int(math.log2(size_tile)))]
    masks = dp_masks + tile_masks
    if core == 1 and len(masks) >= 2:
        masks = [masks[1], masks[0]] + masks[2:]
    return masks


def part_order(me_dp, me_tile, size_dp, size_tile, levels):
    core = me_tile & 1
    kept = []
    for which in (0, 1):
        value = 0
        for dm, tm in step_masks(size_dp, size_tile, which)[: levels - 1]:
            bit = ((me_dp & dm) | (me_tile & tm)) != 0
            value = 2 * value + bit.astype(jnp.int32)
        kept.append(value)
    top = 1 << (levels - 1)
    places = jnp.arange(top, dtype=jnp.int32)
    same = (places ^ jnp.where(core == 0, kept[0], kept[1])) + core * top
    flipped = (places ^ jnp.where(core == 0, kept[1], kept[0])) + (1 - core) * top
    return jnp.concatenate([same, flipped])


def region_sum(terms, axis, low, high):
    total = lax.slice_in_dim(terms[0], low, high, axis=axis).astype(F32)
    for term in terms[1:]:
        total = total + lax.slice_in_dim(term, low, high, axis=axis).astype(F32)
    return total


class Chain:
    def __init__(self, keep, send, sizes, levels, scale):
        self.sizes = sizes
        self.masks = [step_masks(*sizes, core) for core in (0, 1)]
        self.steps = len(self.masks[0])
        self.levels = levels
        self.scale = scale
        self.terms = [keep]
        self.sent = send
        self.recv = None
        self.extent = keep.shape[1]
        self.count = 1 + self.steps + levels
        self.done = 0

    def total(self):
        if self.done <= self.levels:
            return region_sum(self.terms[:-1] + [self.recv], 1, 0, self.extent)
        return self.sent.astype(F32) + self.recv.astype(F32)

    def step(self, *after):
        n = self.done
        which = n
        if n == 0:
            send = self.sent
        elif n < self.levels:
            self.terms[-1] = self.recv
            send = region_sum(self.terms, 1, self.extent // 2, self.extent).astype(BF16)
            self.extent //= 2
        elif n <= self.steps:
            send = self.total().astype(BF16)
        else:
            which = self.levels - (n - self.steps)
            if n == self.steps + 1:
                send = (self.total() * self.scale).astype(BF16)
            else:
                send = jnp.concatenate([self.sent, self.recv], axis=1)
        if after:
            send = together(send, *after)[0]
        flip = lambda core: (0, 1) if which == 0 else self.masks[core][which - 1]
        self.sent = send
        self.recv = exchange(send, *self.sizes, flip)
        if n < self.levels:
            self.terms.append(self.recv)
        self.done += 1

    def more(self):
        return self.done < self.count

    def tie(self, value):
        self.recv, value = together(self.recv, value)
        return value


def place_kernel(halves, order_ref, info_ref, *refs):
    out_ref = refs[-1]
    parts = order_ref.shape[0]
    size = out_ref.shape[1] // (len(halves) * parts // 2)
    for source_ref, half in zip(refs, halves):
        for s in range(parts // 2):
            place = order_ref[half * (parts // 2) + s]
            if len(halves) == 1:
                place = place & (parts // 2 - 1)
            target = pl.multiple_of(place * size, size)
            out_ref[:, pl.ds(target, size), :] = source_ref[:, s * size : (s + 1) * size, :]


def place_parts(order, info, halves, sources, blocks, count, before):
    taps, rows, chans = sources[0].shape
    group = taps // len(blocks)

    def target(t, order_ref, info_ref):
        side = (info_ref[0] & 1) ^ halves[0] if len(halves) == 1 else 0
        return (pick(t, blocks), side, 0)

    return pl.pallas_call(
        functools.partial(place_kernel, halves),
        grid_spec=pltpu.PrefetchScalarGridSpec(
            num_scalar_prefetch=2,
            grid=(len(blocks),),
            in_specs=[pl.BlockSpec((group, rows, chans), lambda t, o, i: (t, 0, 0))] * len(sources)
            + [ANY] * len(before),
            out_specs=pl.BlockSpec((group, len(halves) * rows, chans), target),
        ),
        out_shape=jax.ShapeDtypeStruct((count, 2 * rows, chans), BF16),
        input_output_aliases={2 + len(sources): 0} if before else {},
        compiler_params=params(),
        cost_estimate=cost(0, 4 * taps * len(halves) * rows * chans),
        name="place_parts",
    )(order, info, *sources, *before)


def together(*values):
    return lax.optimization_barrier(values)


def body(grad_out, bev_act, conv_weight, img_in, backbone_weight, route, offsets, frac_x, frac_y):
    tiles = lax.axis_size("tile")
    pods = lax.axis_size("dp")
    my_tile = lax.axis_index("tile")
    my_pod = lax.axis_index("dp")
    grad = grad_out[0]
    rows, cols, chans = grad.shape
    image = img_in[0]
    weight = jnp.transpose(conv_weight, (1, 2, 0, 3))
    per = image.shape[0] // (2 * IMGW)
    own = rows * cols // BLK
    edge_blocks = cols // BLK
    steps = int(math.log2(pods * tiles))
    levels = min(CONV_LEVELS, steps, int(math.log2(chans // 16)))
    back_levels = min(2, levels)
    order = part_order(my_pod, my_tile, pods, tiles, levels)
    back_order = part_order(my_pod, my_tile, pods, tiles, back_levels)
    cell_scale = 1.0 / math.sqrt(pods * tiles * rows * cols)
    pixel_scale = 1.0 / math.sqrt(pods * tiles * image.shape[0])

    forward = [(i, i + 1) for i in range(tiles - 1)]
    backward = [(b, a) for a, b in forward]
    low = lax.ppermute(grad[rows - 1], "tile", forward)
    high = lax.ppermute(grad[0], "tile", backward)

    core_swap = [(t, t ^ 1) for t in range(tiles)]
    cells = jnp.stack([offsets[0], frac_x[0], frac_y[0]]).reshape(3, own, BLK)
    cells_other = lax.ppermute(cells, "tile", core_swap)

    info = jnp.reshape(my_tile, (1,)).astype(jnp.int32)
    inner = bev_rows(grad, [], weight, tuple(range(1, rows - 1)), [])
    inner_other = lax.ppermute(inner, "tile", core_swap)
    sizes = (pods, tiles)
    act = bev_act[0]
    edge = bev_rows(grad, [low, high], weight, (0, rows - 1), [inner, cells_other])
    edge_other = lax.ppermute(edge, "tile", core_swap)
    slope = image_slope(image, backbone_weight, [edge])
    as_blocks = lambda value: value.reshape(-1, BLK, chans)
    keep, send = warp_pieces(
        info,
        route[0],
        cells,
        cells_other,
        [as_blocks(v) for v in (inner, edge, inner_other, edge_other)],
        tiles,
        per,
        edge_blocks,
        [slope],
    )

    tile_masks = [(0, 1 << n) for n in range(1, int(math.log2(tiles)))]
    swapped = [tile_masks[1], tile_masks[0]] + tile_masks[2:] if len(tile_masks) > 1 else tile_masks
    warp_masks = (tile_masks, swapped)
    warp = [keep]
    extent = keep.shape[0]
    last = len(tile_masks) - 1

    def warp_step(n, send):
        nonlocal extent
        if n > 0:
            send = region_sum(warp, 0, extent // 2, extent).astype(BF16)
            extent //= 2
        warp.append(exchange(send, *sizes, lambda core: warp_masks[core][n]))

    warp_step(0, send)
    early_taps = tuple((i, j) for j in (1, 0, 2) for i in (1, 0))
    late_taps = tuple((2, j) for j in (1, 0, 2))
    outs = wgrad(
        order, act, grad, [low, high], early_taps, tuple(3 * i + j for i, j in early_taps), 6, [], [keep]
    )
    early = Chain(*outs, sizes, levels, cell_scale)
    early.step()
    outs = list(wgrad(order, act, grad, [low, high], late_taps, (1, 0, 2), 3, [], [outs[0]]))
    outs[0] = early.tie(outs[0])
    late = Chain(*outs, sizes, levels, cell_scale)
    warp[1], late.sent = together(warp[1], late.sent)

    warp_step(1, None)
    late.step()
    early.step(warp[1])
    warp[2] = late.tie(warp[2])

    warp_step(2, None)
    late.step(warp[2])
    early.step()
    late.step()
    warp[3] = early.tie(warp[3])
    warp[3] = late.tie(warp[3])
    for n in range(3, last + 1):
        warp_step(n, None)

    image_grad, keep_img, send_img = image_layer(back_order, [warp], slope, image, backbone_weight)
    back = Chain(keep_img, send_img, sizes, back_levels, pixel_scale)
    chains = [back, early, late]
    before = [send_img]
    while any(chain.more() for chain in chains):
        for chain in chains:
            if chain.more():
                held = chain.recv
                chain.step(*before)
                before = [] if held is None else [held]

    conv_grad = place_parts(order, info, (0,), [early.sent], (0, 1), 9, [])
    conv_grad = place_parts(order, info, (1,), [early.recv], (0, 1), 9, [conv_grad])
    conv_grad = place_parts(order, info, (0, 1), [late.sent, late.recv], (2,), 9, [conv_grad])
    backbone_grad = place_parts(back_order, info, (0, 1), [back.sent, back.recv], (0,), 1, [])[0]
    conv_grad = jnp.transpose(conv_grad.reshape(3, 3, chans, chans), (2, 0, 1, 3))
    return (image_grad[None], conv_grad, backbone_grad)


def solution(mesh):
    return jax.shard_map(
        body,
        mesh=mesh,
        in_specs=(
            P("dp", "tile", None, None),
            P("dp", "tile", None, None),
            P(),
            P("dp", "tile", None),
            P(),
            P("dp", None),
            P("dp", "tile"),
            P("dp", "tile"),
            P("dp", "tile"),
        ),
        out_specs=(P("dp", "tile", None), P(), P()),
        check_vma=False,
    )
```

```python
import functools
import math

import jax
import jax.numpy as jnp
from jax import lax
from jax.experimental import pallas as pl
from jax.experimental.pallas import tpu as pltpu
from jax.sharding import PartitionSpec as P

BLK = 64
IMGW = 64
GROUP = 4
BATCH = 4
EARLY_LEVELS = 4
LATE_LEVELS = 3
BACK_LEVELS = 2
VMEM_BYTES = 63 * 1024 * 1024
F32 = jnp.float32
BF16 = jnp.bfloat16
VMEM = pl.BlockSpec(memory_space=pltpu.VMEM)
SMEM = pl.BlockSpec(memory_space=pltpu.SMEM)
ANY = pl.BlockSpec(memory_space=pl.ANY)


def params(**extra):
    return pltpu.CompilerParams(vmem_limit_bytes=VMEM_BYTES, **extra)


def cost(flops, nbytes):
    return pl.CostEstimate(flops=int(flops), bytes_accessed=int(nbytes), transcendentals=0)


def nt_dot(a, b):
    return lax.dot_general(a, b, (((1,), (1,)), ((), ())), preferred_element_type=F32)


def column_shift(value, by):
    if by == 0:
        return value
    length = value.shape[0]
    place = lax.broadcasted_iota(jnp.int32, value.shape, 0)
    edge = length - 1 if by > 0 else 0
    return jnp.where(place == edge, 0.0, pltpu.roll(value, (-by) % length, 0))


def bev_kernel(targets, halo, g_ref, *refs):
    if halo:
        low_ref, high_ref = refs[:2]
        refs = refs[2:]
    w_ref, out_ref, acc_ref = refs
    rows = g_ref.shape[0]
    step = pl.program_id(0)

    def frame(u):
        if u < 0:
            return low_ref[...]
        if u >= rows:
            return high_ref[...]
        return g_ref[u]

    for order, j in enumerate((1, 0, 2)):
        @pl.when(step == order)
        def _(j=j, order=order):
            rhs = jnp.concatenate([w_ref[i, 0] for i in range(3)], axis=1)
            for n, u in enumerate(targets):
                lhs = jnp.concatenate([frame(u - i + 1) for i in range(3)], axis=1)
                term = column_shift(nt_dot(lhs, rhs), 1 - j)
                if order == 0:
                    acc_ref[n] = term
                elif order == 1:
                    acc_ref[n] = acc_ref[n] + term
                else:
                    out_ref[n] = (acc_ref[n] + term).astype(BF16)


def col_tap(step):
    return jnp.where(step == 0, 1, jnp.where(step == 1, 0, 2))


def bev_rows(grad, halos, weight, targets, after):
    rows, cols, chans = grad.shape
    whole = lambda *shape: pl.BlockSpec(shape, lambda s: (0,) * len(shape))
    count = len(targets)

    def kernel(g_ref, *refs):
        n = len(halos) + 1
        bev_kernel(targets, len(halos) > 0, g_ref, *refs[:n], *refs[n + len(after) :])

    return pl.pallas_call(
        kernel,
        grid=(3,),
        in_specs=[whole(rows, cols, chans)]
        + [whole(cols, chans)] * len(halos)
        + [pl.BlockSpec((3, 1, chans, chans), lambda s: (0, col_tap(s), 0, 0))]
        + [ANY] * len(after),
        out_specs=whole(count, cols, chans),
        out_shape=jax.ShapeDtypeStruct((count, cols, chans), BF16),
        scratch_shapes=[pltpu.VMEM((count, cols, chans), F32)],
        compiler_params=params(),
        cost_estimate=cost(18 * count * cols * chans * chans, 2 * (2 * rows * cols * chans + 9 * chans * chans)),
        name="bev_rows",
    )(grad, *halos, weight, *after)


def tn_dot(a, b):
    return lax.dot_general(a, b, (((0,), (0,)), ((), ())), preferred_element_type=F32)


def spread(value_ref, order_ref, keep_ref, send_ref):
    parts = order_ref.shape[0]
    size = value_ref.shape[0] // parts
    for half, target in enumerate((keep_ref, send_ref)):
        for s in range(parts // 2):
            source = pl.multiple_of(order_ref[half * (parts // 2) + s] * size, size)
            target[0, s * size : (s + 1) * size, :] = value_ref[pl.ds(source, size), :].astype(BF16)


def wgrad_kernel(taps, halo, order_ref, a_ref, g_ref, *refs):
    if halo:
        low_ref, high_ref = refs[:2]
    keep_ref, send_ref, moved_ref, wide_ref = refs[-4:]
    rows, cols, chans = a_ref.shape
    total = rows * cols
    step = pl.program_id(0)
    for t, (i, j) in enumerate(taps):
        fresh = j != 1 and (t == 0 or taps[t - 1][1] != j)

        @pl.when(step == t)
        def _(i=i, j=j, fresh=fresh):
            if fresh:
                for u in range(rows):
                    moved_ref[u * cols : (u + 1) * cols, :] = column_shift(
                        a_ref[u].astype(F32), j - 1
                    ).astype(BF16)
            if j == 1:
                act = lambda low, high: a_ref[low:high].reshape((high - low) * cols, chans)
            else:
                act = lambda low, high: moved_ref[low * cols : high * cols, :]
            if i == 1:
                wide_ref[...] = tn_dot(act(0, rows), g_ref[...])
            elif i == 0:
                wide_ref[...] = tn_dot(act(0, rows - 1), g_ref[cols:, :]) + tn_dot(
                    act(rows - 1, rows), high_ref[...]
                )
            else:
                wide_ref[...] = tn_dot(act(1, rows), g_ref[: total - cols, :]) + tn_dot(
                    act(0, 1), low_ref[...]
                )
            spread(wide_ref, order_ref, keep_ref, send_ref)


def pick(index, values):
    result = values[0]
    for n, value in enumerate(values):
        result = jnp.where(index == n, value, result)
    return result


def wgrad(order, act, grad, halos, taps, places, count, before, after):
    rows, cols, chans = grad.shape
    whole = lambda *shape: pl.BlockSpec(shape, lambda t: (0,) * len(shape))
    half_spec = pl.BlockSpec((1, chans // 2, chans), lambda t: (pick(t, places), 0, 0))
    shape = jax.ShapeDtypeStruct((count, chans // 2, chans), BF16)
    ahead = 3 + len(halos)
    return pl.pallas_call(
        functools.partial(wgrad_kernel, taps, len(halos) > 0),
        grid=(len(taps),),
        in_specs=[SMEM, whole(rows, cols, chans), whole(rows * cols, chans)]
        + [whole(cols, chans)] * len(halos)
        + [ANY] * (len(before) + len(after)),
        out_specs=[half_spec, half_spec],
        out_shape=[shape, shape],
        scratch_shapes=[pltpu.VMEM((rows * cols, chans), BF16), pltpu.VMEM((chans, chans), F32)],
        input_output_aliases={ahead: 0, ahead + 1: 1} if before else {},
        compiler_params=params(),
        cost_estimate=cost(
            2 * len(taps) * rows * cols * chans * chans,
            2 * (2 * rows * cols * chans + len(taps) * chans * chans),
        ),
        name="wgrad",
    )(order, act, grad.reshape(rows * cols, chans), *halos, *before, *after)


def pieces_kernel(
    plan, info_ref, route_ref, mine_ref, other_ref, *refs
):
    own_blocks, per, tile_bits, edge, after = plan
    sources = refs[:4]
    outs = refs[4 + after : 6 + after]
    blocks_ref, cells_ref, acc_ref, count_ref, list_ref, sems = refs[6 + after :]
    off_ref, fx_ref, fy_ref = cells_ref.at[0], cells_ref.at[1], cells_ref.at[2]
    copies = []
    start = 0
    for n, source in enumerate(sources):
        size = source.shape[0]
        copies.append(pltpu.make_async_copy(source, blocks_ref.at[pl.ds(start, size)], sems.at[n]))
        start += size
    for copy in copies:
        copy.start()
    for n in range(3):
        for start, cells in ((0, mine_ref), (own_blocks, other_ref)):
            cells_ref[n, start : start + own_blocks, :] = jnp.concatenate([cells[n], cells[n]], axis=1)
    tile = info_ref[0]
    core = tile & 1
    slots = outs[0].shape[0] * 2
    wide = 2 * own_blocks
    inner = own_blocks - 2 * edge

    @pl.loop(0, slots * per)
    def _(n):
        count_ref[n] = 0
        for g in range(GROUP):
            list_ref[n * wide + g] = wide

    per_bits = int(math.log2(per))
    for other in range(2):
        for first, last, shift in (
            (0, edge, inner),
            (edge, own_blocks - edge, -edge),
            (own_blocks - edge, own_blocks, 0),
        ):
            @pl.loop(first, last)
            def _(k, other=other, shift=shift):
                ident = route_ref[0, (tile ^ other) * own_blocks + k]
                owner = ident >> per_bits
                local = ident & (per - 1)

                @pl.when(((owner ^ tile) & 1) == 0)
                def _():
                    at = slot_of((owner ^ tile) >> 1, core, tile_bits) * per + local
                    have = count_ref[at]
                    spot = other * own_blocks + shift + k
                    list_ref[at * wide + have] = (spot << 16) + (other * own_blocks + k)
                    count_ref[at] = have + 1

    cells_ref[0, wide : wide + 8, :] = jnp.full((8, 2 * BLK), -2 * IMGW, jnp.int32)
    for n in range(1, 3):
        cells_ref[n, wide : wide + 8, :] = jnp.zeros((8, 2 * BLK), jnp.int32)

    for copy in copies:
        copy.wait()

    lanes = lax.broadcasted_iota(jnp.int32, (1, 2 * BLK), 1)
    low_lane = lanes < BLK

    def group_product(entries):
        picked = [(entry & 0xFFFF, entry >> 16) for entry in entries]
        rhs = jnp.concatenate([blocks_ref[spot] for _, spot in picked], axis=0)

        def lane_row(ref):
            halves = []
            for p in range(0, GROUP, 2):
                a = ref[pl.ds(picked[p][0], 1), :]
                b = ref[pl.ds(picked[p + 1][0], 1), :]
                halves.append(jnp.where(low_lane, a, b))
            return jnp.concatenate(halves, axis=1)

        left = lane_row(off_ref)
        right_w = lane_row(fx_ref).astype(F32) / 256.0
        lower_w = lane_row(fy_ref).astype(F32) / 256.0
        column = lax.broadcasted_iota(jnp.int32, (IMGW, GROUP * BLK), 0)
        across = jnp.where(column == left, 1.0 - right_w, 0.0) + jnp.where(
            column == left + 1, right_w, 0.0
        )
        band = jnp.concatenate([(1.0 - lower_w) * across, lower_w * across], axis=0).astype(BF16)
        return jnp.dot(band, rhs, preferred_element_type=F32)

    def overfill(out, at, inside):
        have = count_ref[at]

        @pl.when(have > GROUP)
        def _():
            acc_ref[...] = jnp.zeros_like(acc_ref)

            @pl.loop(0, (have + GROUP - 1) // GROUP)
            def _(m):
                entries = []
                for g in range(GROUP):
                    index = m * GROUP + g
                    entry = list_ref[at * wide + jnp.minimum(index, wide - 1)]
                    entries.append(jnp.where(index < have, entry, wide))
                acc_ref[...] = acc_ref[...] + group_product(entries)

            out[inside[0], inside[1]] = acc_ref[...].astype(BF16)

    for half in (1, 0):
        out = outs[half]
        base = half * (slots // 2)

        @pl.loop(0, (slots // 2) * per // BATCH)
        def _(m, out=out, base=base):
            values = []
            for n in range(BATCH):
                at = base * per + m * BATCH + n
                entries = [list_ref[at * wide + g] for g in range(GROUP)]
                values.append(group_product(entries).astype(BF16))
            for n in range(BATCH):
                spot = m * BATCH + n
                out[spot >> per_bits, spot & (per - 1)] = values[n]

        @pl.loop(0, (slots // 2) * per)
        def _(spot, out=out, base=base):
            overfill(out, base * per + spot, (spot >> per_bits, spot & (per - 1)))


def swap_low_bits(value):
    return (value & ~3) | ((value & 1) << 1) | ((value >> 1) & 1)


def slot_of(away, core, bits):
    place = 0
    first = jnp.where((core == 1) & (bits >= 2), swap_low_bits(away), away)
    for n in range(bits):
        place = place | (((first >> n) & 1) << (bits - 1 - n))
    return place


def warp_pieces(info, route, cells, cells_other, sources, tiles, per, edge, after):
    own = sources[0].shape[0] + sources[1].shape[0]
    chans = sources[0].shape[2]
    bits = int(math.log2(tiles)) - 1
    slots = tiles // 2
    shape = jax.ShapeDtypeStruct((slots // 2, per, 2 * IMGW, chans), BF16)
    return pl.pallas_call(
        functools.partial(pieces_kernel, (own, per, bits, edge, len(after))),
        in_specs=[SMEM, SMEM, VMEM, VMEM] + [ANY] * (4 + len(after)),
        out_specs=[VMEM] * 2,
        out_shape=[shape] * 2,
        scratch_shapes=[
            pltpu.VMEM((2 * own, BLK, chans), BF16),
            pltpu.VMEM((3, 2 * own + 8, 2 * BLK), jnp.int32),
            pltpu.VMEM((2 * IMGW, chans), F32),
            pltpu.SMEM((slots * per,), jnp.int32),
            pltpu.SMEM((slots * per * 2 * own,), jnp.int32),
            pltpu.SemaphoreType.DMA((4,)),
        ],
        compiler_params=params(),
        cost_estimate=cost(
            2 * slots * per * 2 * IMGW * GROUP * BLK * chans, 2 * (own * 2 * BLK * chans + slots * per * 2 * IMGW * chans)
        ),
        name="warp_pieces",
    )(info, route, cells, cells_other, *sources, *after)


def slope_kernel(img_ref, w_ref, *refs):
    slope_ref = refs[-1]
    value = jnp.dot(img_ref[...], w_ref[...], preferred_element_type=F32)
    sigma = jax.nn.sigmoid(value)
    slope_ref[...] = sigma * (1.0 + value * (1.0 - sigma))


def image_slope(image, weight, after):
    pixels, chans = image.shape
    return pl.pallas_call(
        slope_kernel,
        in_specs=[VMEM, VMEM] + [ANY] * len(after),
        out_specs=VMEM,
        out_shape=jax.ShapeDtypeStruct((pixels, chans), F32),
        compiler_params=params(),
        cost_estimate=cost(2 * pixels * chans * chans, 10 * pixels * chans),
        name="image_slope",
    )(image, weight, *after)


def image_kernel(chunks, order_ref, *refs):
    terms = refs[: sum(chunks)]
    slope_ref, image_ref, w_ref, img_out, keep_ref, send_ref, wide_ref = refs[sum(chunks) :]
    feature = []
    start = 0
    for size in chunks:
        total = terms[start][0].astype(F32)
        for term in terms[start + 1 : start + size]:
            total = total + term[0].astype(F32)
        feature.append(total.reshape(-1, total.shape[-1]))
        start += size
    feature = jnp.concatenate(feature, axis=0)
    scaled = (feature * slope_ref[...]).astype(BF16)
    wide_ref[...] = tn_dot(image_ref[...], scaled)
    spread(wide_ref, order_ref, keep_ref, send_ref)
    img_out[...] = nt_dot(scaled, w_ref[...]).astype(BF16)


def image_layer(order, chunks, slope, image, weight):
    pixels, chans = slope.shape
    half = jax.ShapeDtypeStruct((1, chans // 2, chans), BF16)
    whole = lambda *shape: pl.BlockSpec(shape, lambda n: (0,) * len(shape))
    terms = [term for chunk in chunks for term in chunk]
    return pl.pallas_call(
        functools.partial(image_kernel, tuple(len(chunk) for chunk in chunks)),
        grid=(1,),
        in_specs=[SMEM]
        + [whole(1, *term.shape[1:]) for term in terms]
        + [whole(pixels, chans), whole(pixels, chans), whole(chans, chans)],
        out_specs=[whole(pixels, chans), whole(1, chans // 2, chans), whole(1, chans // 2, chans)],
        out_shape=[jax.ShapeDtypeStruct((pixels, chans), BF16), half, half],
        scratch_shapes=[pltpu.VMEM((chans, chans), F32)],
        compiler_params=params(),
        cost_estimate=cost(4 * pixels * chans * chans, 16 * pixels * chans),
        name="image_layer",
    )(order, *terms, slope, image, weight)


def exchange(value, size_dp, size_tile, flip):
    pairs = []
    for d in range(size_dp):
        for t in range(size_tile):
            dm, tm = flip(t & 1)
            pairs.append((d * size_tile + t, (d ^ dm) * size_tile + (t ^ tm)))
    return lax.ppermute(value, ("dp", "tile"), pairs)


def step_masks(size_dp, size_tile, core):
    dp_masks = [(1 << n, 0) for n in range(int(math.log2(size_dp)))]
    tile_masks = [(0, 1 << n) for n in range(1, int(math.log2(size_tile)))]
    masks = dp_masks + tile_masks
    if core == 1 and len(masks) >= 2:
        masks = [masks[1], masks[0]] + masks[2:]
    return masks


def part_order(me_dp, me_tile, size_dp, size_tile, levels):
    core = me_tile & 1
    kept = []
    for which in (0, 1):
        value = 0
        for dm, tm in step_masks(size_dp, size_tile, which)[: levels - 1]:
            bit = ((me_dp & dm) | (me_tile & tm)) != 0
            value = 2 * value + bit.astype(jnp.int32)
        kept.append(value)
    top = 1 << (levels - 1)
    places = jnp.arange(top, dtype=jnp.int32)
    same = (places ^ jnp.where(core == 0, kept[0], kept[1])) + core * top
    flipped = (places ^ jnp.where(core == 0, kept[1], kept[0])) + (1 - core) * top
    return jnp.concatenate([same, flipped])


def region_sum(terms, axis, low, high):
    total = lax.slice_in_dim(terms[0], low, high, axis=axis).astype(F32)
    for term in terms[1:]:
        total = total + lax.slice_in_dim(term, low, high, axis=axis).astype(F32)
    return total


class Chain:
    def __init__(self, keep, send, sizes, levels, scale):
        self.sizes = sizes
        self.masks = [step_masks(*sizes, core) for core in (0, 1)]
        self.steps = len(self.masks[0])
        self.levels = levels
        self.scale = scale
        self.terms = [keep]
        self.sent = send
        self.recv = None
        self.extent = keep.shape[1]
        self.count = 1 + self.steps + levels
        self.done = 0

    def total(self):
        if self.done <= self.levels:
            return region_sum(self.terms[:-1] + [self.recv], 1, 0, self.extent)
        return self.sent.astype(F32) + self.recv.astype(F32)

    def step(self, *after):
        n = self.done
        which = n
        if n == 0:
            send = self.sent
        elif n < self.levels:
            self.terms[-1] = self.recv
            send = region_sum(self.terms, 1, self.extent // 2, self.extent).astype(BF16)
            self.extent //= 2
        elif n <= self.steps:
            send = self.total().astype(BF16)
        else:
            which = self.levels - (n - self.steps)
            if n == self.steps + 1:
                send = (self.total() * self.scale).astype(BF16)
            else:
                send = jnp.concatenate([self.sent, self.recv], axis=1)
        if after:
            send = together(send, *after)[0]
        flip = lambda core: (0, 1) if which == 0 else self.masks[core][which - 1]
        self.sent = send
        self.recv = exchange(send, *self.sizes, flip)
        if n < self.levels:
            self.terms.append(self.recv)
        self.done += 1

    def more(self):
        return self.done < self.count

    def tie(self, value):
        self.recv, value = together(self.recv, value)
        return value


def place_kernel(spans, *refs):
    tables = refs[: len(spans)]
    sources = refs[len(spans) : 3 * len(spans)]
    conv_ref, back_ref = refs[3 * len(spans) :]
    step = pl.program_id(0)
    start = 0
    for n, span in enumerate(spans):
        out_ref = back_ref if n == len(spans) - 1 else conv_ref
        parts = tables[n].shape[0]
        size = out_ref.shape[1] // parts

        @pl.when((step >= start) & (step < start + span))
        def _(n=n, out_ref=out_ref, parts=parts, size=size):
            for half in range(2):
                for s in range(parts // 2):
                    place = tables[n][half * (parts // 2) + s]
                    target = pl.multiple_of(place * size, size)
                    out_ref[:, pl.ds(target, size), :] = sources[2 * n + half][
                        :, s * size : (s + 1) * size, :
                    ]

        start += span


def place_parts(tables, chunks):
    chans = chunks[0][0].shape[2]
    spans = tuple(max(1, mine.shape[0] // 3) for mine, _ in chunks)
    starts = [sum(spans[:n]) for n in range(len(spans))]
    groups = sum(spans) - 1
    in_specs = [SMEM] * len(tables)
    for (mine, _), span, start in zip(chunks, spans, starts):
        block = (mine.shape[0] // span,) + mine.shape[1:]
        index = lambda t, span=span, start=start: (jnp.clip(t - start, 0, span - 1), 0, 0)
        in_specs += [pl.BlockSpec(block, index)] * 2
    return pl.pallas_call(
        functools.partial(place_kernel, spans),
        grid=(sum(spans),),
        in_specs=in_specs,
        out_specs=[
            pl.BlockSpec((3, chans, chans), lambda t: (jnp.minimum(t, groups - 1), 0, 0)),
            pl.BlockSpec((1, chans, chans), lambda t: (0, 0, 0)),
        ],
        out_shape=[
            jax.ShapeDtypeStruct((3 * groups, chans, chans), BF16),
            jax.ShapeDtypeStruct((1, chans, chans), BF16),
        ],
        compiler_params=params(),
        cost_estimate=cost(0, 40 * chans * chans),
        name="place_parts",
    )(*tables, *[half for chunk in chunks for half in chunk])


def together(*values):
    return lax.optimization_barrier(values)


def body(grad_out, bev_act, conv_weight, img_in, backbone_weight, route, offsets, frac_x, frac_y):
    tiles = lax.axis_size("tile")
    pods = lax.axis_size("dp")
    my_tile = lax.axis_index("tile")
    my_pod = lax.axis_index("dp")
    grad = grad_out[0]
    rows, cols, chans = grad.shape
    image = img_in[0]
    weight = jnp.transpose(conv_weight, (1, 2, 0, 3))
    per = image.shape[0] // (2 * IMGW)
    own = rows * cols // BLK
    edge_blocks = cols // BLK
    steps = int(math.log2(pods * tiles))
    most = min(steps, int(math.log2(chans // 16)))
    early_levels, late_levels, back_levels = (
        min(levels, most) for levels in (EARLY_LEVELS, LATE_LEVELS, BACK_LEVELS)
    )
    order_of = lambda levels: part_order(my_pod, my_tile, pods, tiles, levels)
    early_order, late_order, back_order = map(order_of, (early_levels, late_levels, back_levels))
    cell_scale = 1.0 / math.sqrt(pods * tiles * rows * cols)
    pixel_scale = 1.0 / math.sqrt(pods * tiles * image.shape[0])

    forward = [(i, i + 1) for i in range(tiles - 1)]
    backward = [(b, a) for a, b in forward]
    low = lax.ppermute(grad[rows - 1], "tile", forward)
    high = lax.ppermute(grad[0], "tile", backward)

    core_swap = [(t, t ^ 1) for t in range(tiles)]
    cells = jnp.stack([offsets[0], frac_x[0], frac_y[0]]).reshape(3, own, BLK)
    cells_other = lax.ppermute(cells, "tile", core_swap)

    info = jnp.reshape(my_tile, (1,)).astype(jnp.int32)
    inner = bev_rows(grad, [], weight, tuple(range(1, rows - 1)), [])
    inner_other = lax.ppermute(inner, "tile", core_swap)
    sizes = (pods, tiles)
    act = bev_act[0]
    edge = bev_rows(grad, [low, high], weight, (0, rows - 1), [inner, cells_other])
    edge_other = lax.ppermute(edge, "tile", core_swap)
    slope = image_slope(image, backbone_weight, [edge])
    as_blocks = lambda value: value.reshape(-1, BLK, chans)
    keep, send = warp_pieces(
        info,
        route,
        cells,
        cells_other,
        [as_blocks(v) for v in (inner, edge, inner_other, edge_other)],
        tiles,
        per,
        edge_blocks,
        [slope],
    )

    tile_masks = [(0, 1 << n) for n in range(1, int(math.log2(tiles)))]
    swapped = [tile_masks[1], tile_masks[0]] + tile_masks[2:] if len(tile_masks) > 1 else tile_masks
    warp_masks = (tile_masks, swapped)
    warp = [keep]
    extent = keep.shape[0]
    last = len(tile_masks) - 1

    def warp_step(n, send):
        nonlocal extent
        if n > 0:
            send = region_sum(warp, 0, extent // 2, extent).astype(BF16)
            extent //= 2
        warp.append(exchange(send, *sizes, lambda core: warp_masks[core][n]))
        return send

    warp_step(0, send)
    early_taps = tuple((i, j) for j in (1, 0, 2) for i in (1, 0))
    late_taps = tuple((2, j) for j in (1, 0, 2))
    outs = wgrad(
        early_order,
        act,
        grad,
        [low, high],
        early_taps,
        tuple(3 * i + j for i, j in early_taps),
        6,
        [],
        [keep],
    )
    early = Chain(*outs, sizes, early_levels, cell_scale)
    early.step()
    outs = list(wgrad(late_order, act, grad, [low, high], late_taps, (1, 0, 2), 3, [], [outs[0]]))
    outs[0] = early.tie(outs[0])
    late = Chain(*outs, sizes, late_levels, cell_scale)
    warp[1], late.sent = together(warp[1], late.sent)

    sent = warp_step(1, None)
    late.step()
    early.step(sent)
    warp[2] = late.tie(warp[2])

    sent = warp_step(2, None)
    early.step(sent)
    late.step(sent)
    for n in range(3, last + 1):
        warp_step(n, None)

    image_grad, keep_img, send_img = image_layer(back_order, [warp], slope, image, backbone_weight)
    back = Chain(keep_img, send_img, sizes, back_levels, pixel_scale)
    early.step()
    early.recv, late.recv, _ = together(early.recv, late.recv, send_img)
    chains = [back, early, late]
    before = [send_img]
    while any(chain.more() for chain in chains):
        for chain in chains:
            if chain.more():
                held = chain.recv
                chain.step(*before)
                before = [] if held is None else [held]

    conv_grad, backbone_grad = place_parts(
        [early_order, late_order, back_order],
        [(chain.sent, chain.recv) for chain in (early, late, back)],
    )
    backbone_grad = backbone_grad[0]
    conv_grad = jnp.transpose(conv_grad.reshape(3, 3, chans, chans), (2, 0, 1, 3))
    return (image_grad[None], conv_grad, backbone_grad)


def solution(mesh):
    return jax.shard_map(
        body,
        mesh=mesh,
        in_specs=(
            P("dp", "tile", None, None),
            P("dp", "tile", None, None),
            P(),
            P("dp", "tile", None),
            P(),
            P("dp", None),
            P("dp", "tile"),
            P("dp", "tile"),
            P("dp", "tile"),
        ),
        out_specs=(P("dp", "tile", None), P(), P()),
        check_vma=False,
    )
```

```python
import functools
import math

import jax
import jax.numpy as jnp
from jax import lax
from jax.experimental import pallas as pl
from jax.experimental.pallas import tpu as pltpu
from jax.sharding import PartitionSpec as P

BLK = 64
IMGW = 64
GROUP = 4
BATCH = 4
EARLY_LEVELS = 4
LATE_LEVELS = 3
BACK_LEVELS = 2
EARLY_WAITS = (0, 0, 0, 0, 0, 2, 3, 4, 6)
LATE_WAITS = (0, 0, 0, 0, 1, 3, 4, 5)
VMEM_BYTES = 63 * 1024 * 1024
F32 = jnp.float32
BF16 = jnp.bfloat16
VMEM = pl.BlockSpec(memory_space=pltpu.VMEM)
SMEM = pl.BlockSpec(memory_space=pltpu.SMEM)
ANY = pl.BlockSpec(memory_space=pl.ANY)


def params(**extra):
    return pltpu.CompilerParams(vmem_limit_bytes=VMEM_BYTES, **extra)


def cost(flops, nbytes):
    return pl.CostEstimate(flops=int(flops), bytes_accessed=int(nbytes), transcendentals=0)


def nt_dot(a, b):
    return lax.dot_general(a, b, (((1,), (1,)), ((), ())), preferred_element_type=F32)


def column_shift(value, by):
    if by == 0:
        return value
    length = value.shape[0]
    place = lax.broadcasted_iota(jnp.int32, value.shape, 0)
    edge = length - 1 if by > 0 else 0
    return jnp.where(place == edge, 0.0, pltpu.roll(value, (-by) % length, 0))


def bev_kernel(targets, halo, g_ref, *refs):
    if halo:
        low_ref, high_ref = refs[:2]
        refs = refs[2:]
    w_ref, out_ref, acc_ref = refs
    rows = g_ref.shape[0]
    step = pl.program_id(0)

    def frame(u):
        if u < 0:
            return low_ref[...]
        if u >= rows:
            return high_ref[...]
        return g_ref[u]

    for order, j in enumerate((1, 0, 2)):
        @pl.when(step == order)
        def _(j=j, order=order):
            rhs = jnp.concatenate([w_ref[i, 0] for i in range(3)], axis=1)
            for n, u in enumerate(targets):
                lhs = jnp.concatenate([frame(u - i + 1) for i in range(3)], axis=1)
                term = column_shift(nt_dot(lhs, rhs), 1 - j)
                if order == 0:
                    acc_ref[n] = term
                elif order == 1:
                    acc_ref[n] = acc_ref[n] + term
                else:
                    out_ref[n] = (acc_ref[n] + term).astype(BF16)


def col_tap(step):
    return jnp.where(step == 0, 1, jnp.where(step == 1, 0, 2))


def bev_rows(grad, halos, weight, targets, after):
    rows, cols, chans = grad.shape
    whole = lambda *shape: pl.BlockSpec(shape, lambda s: (0,) * len(shape))
    count = len(targets)

    def kernel(g_ref, *refs):
        n = len(halos) + 1
        bev_kernel(targets, len(halos) > 0, g_ref, *refs[:n], *refs[n + len(after) :])

    return pl.pallas_call(
        kernel,
        grid=(3,),
        in_specs=[whole(rows, cols, chans)]
        + [whole(cols, chans)] * len(halos)
        + [pl.BlockSpec((3, 1, chans, chans), lambda s: (0, col_tap(s), 0, 0))]
        + [ANY] * len(after),
        out_specs=whole(count, cols, chans),
        out_shape=jax.ShapeDtypeStruct((count, cols, chans), BF16),
        scratch_shapes=[pltpu.VMEM((count, cols, chans), F32)],
        compiler_params=params(),
        cost_estimate=cost(18 * count * cols * chans * chans, 2 * (2 * rows * cols * chans + 9 * chans * chans)),
        name="bev_rows",
    )(grad, *halos, weight, *after)


def tn_dot(a, b):
    return lax.dot_general(a, b, (((0,), (0,)), ((), ())), preferred_element_type=F32)


def spread(value_ref, order_ref, keep_ref, send_ref):
    parts = order_ref.shape[0]
    size = value_ref.shape[0] // parts
    for half, target in enumerate((keep_ref, send_ref)):
        for s in range(parts // 2):
            source = pl.multiple_of(order_ref[half * (parts // 2) + s] * size, size)
            target[0, s * size : (s + 1) * size, :] = value_ref[pl.ds(source, size), :].astype(BF16)


def wgrad_kernel(taps, groups, *refs):
    count = max(groups) + 1
    orders = refs[:count]
    a_ref, g_ref, low_ref, high_ref = refs[count : count + 4]
    outs = refs[-2 * count - 2 : -2]
    moved_ref, wide_ref = refs[-2:]
    rows, cols, chans = a_ref.shape
    total = rows * cols
    step = pl.program_id(0)
    for t, (i, j) in enumerate(taps):
        fresh = j != 1 and (t == 0 or taps[t - 1][1] != j)

        @pl.when(step == t)
        def _(i=i, j=j, fresh=fresh, group=groups[t]):
            if fresh:
                for u in range(rows):
                    moved_ref[u * cols : (u + 1) * cols, :] = column_shift(
                        a_ref[u].astype(F32), j - 1
                    ).astype(BF16)
            if j == 1:
                act = lambda low, high: a_ref[low:high].reshape((high - low) * cols, chans)
            else:
                act = lambda low, high: moved_ref[low * cols : high * cols, :]
            if i == 1:
                wide_ref[...] = tn_dot(act(0, rows), g_ref[...])
            elif i == 0:
                wide_ref[...] = tn_dot(act(0, rows - 1), g_ref[cols:, :]) + tn_dot(
                    act(rows - 1, rows), high_ref[...]
                )
            else:
                wide_ref[...] = tn_dot(act(1, rows), g_ref[: total - cols, :]) + tn_dot(
                    act(0, 1), low_ref[...]
                )
            spread(wide_ref, orders[group], *outs[2 * group : 2 * group + 2])


def pick(index, values):
    result = values[0]
    for n, value in enumerate(values):
        result = jnp.where(index == n, value, result)
    return result


def wgrad(orders, act, grad, halos, taps, groups, places, after):
    rows, cols, chans = grad.shape
    whole = lambda *shape: pl.BlockSpec(shape, lambda t: (0,) * len(shape))
    out_specs, out_shape = [], []
    for group in range(len(orders)):
        mine = [n for n in range(len(taps)) if groups[n] == group]
        visited = [places[max([n for n in mine if n <= t], default=mine[0])] for t in range(len(taps))]
        spec = pl.BlockSpec(
            (1, chans // 2, chans), lambda t, visited=visited: (pick(t, visited), 0, 0)
        )
        shape = jax.ShapeDtypeStruct((len(mine), chans // 2, chans), BF16)
        out_specs += [spec, spec]
        out_shape += [shape, shape]
    return pl.pallas_call(
        functools.partial(wgrad_kernel, taps, groups),
        grid=(len(taps),),
        in_specs=[SMEM] * len(orders)
        + [whole(rows, cols, chans), whole(rows * cols, chans)]
        + [whole(cols, chans)] * 2
        + [ANY] * len(after),
        out_specs=out_specs,
        out_shape=out_shape,
        scratch_shapes=[pltpu.VMEM((rows * cols, chans), BF16), pltpu.VMEM((chans, chans), F32)],
        compiler_params=params(),
        cost_estimate=cost(
            2 * len(taps) * rows * cols * chans * chans,
            2 * (2 * rows * cols * chans + len(taps) * chans * chans),
        ),
        name="wgrad",
    )(*orders, act, grad.reshape(rows * cols, chans), *halos, *after)


def pieces_kernel(
    plan, info_ref, route_ref, mine_ref, other_ref, *refs
):
    own_blocks, per, tile_bits, edge, after = plan
    sources = refs[:4]
    outs = refs[4 + after : 8 + after]
    blocks_ref, cells_ref, acc_ref, count_ref, list_ref, sems = refs[8 + after :]
    off_ref, fx_ref, fy_ref = cells_ref.at[0], cells_ref.at[1], cells_ref.at[2]
    copies = []
    start = 0
    for n, source in enumerate(sources):
        size = source.shape[0]
        copies.append(pltpu.make_async_copy(source, blocks_ref.at[pl.ds(start, size)], sems.at[n]))
        start += size
    for copy in copies:
        copy.start()
    for n in range(3):
        for start, cells in ((0, mine_ref), (own_blocks, other_ref)):
            cells_ref[n, start : start + own_blocks, :] = jnp.concatenate([cells[n], cells[n]], axis=1)
    tile = info_ref[0]
    core = tile & 1
    slots = outs[0].shape[0] * 2
    wide = 2 * own_blocks
    inner = own_blocks - 2 * edge

    @pl.loop(0, slots * per)
    def _(n):
        count_ref[n] = 0
        for g in range(GROUP):
            list_ref[n * wide + g] = wide

    per_bits = int(math.log2(per))
    for other in range(2):
        for first, last, shift in (
            (0, edge, inner),
            (edge, own_blocks - edge, -edge),
            (own_blocks - edge, own_blocks, 0),
        ):
            @pl.loop(first, last)
            def _(k, other=other, shift=shift):
                ident = route_ref[0, (tile ^ other) * own_blocks + k]
                owner = ident >> per_bits
                local = ident & (per - 1)

                @pl.when(((owner ^ tile) & 1) == 0)
                def _():
                    at = slot_of((owner ^ tile) >> 1, core, tile_bits) * per + local
                    have = count_ref[at]
                    spot = other * own_blocks + shift + k
                    list_ref[at * wide + have] = (spot << 16) + (other * own_blocks + k)
                    count_ref[at] = have + 1

    cells_ref[0, wide : wide + 8, :] = jnp.full((8, 2 * BLK), -2 * IMGW, jnp.int32)
    for n in range(1, 3):
        cells_ref[n, wide : wide + 8, :] = jnp.zeros((8, 2 * BLK), jnp.int32)

    for copy in copies:
        copy.wait()

    lanes = lax.broadcasted_iota(jnp.int32, (1, 2 * BLK), 1)
    low_lane = lanes < BLK

    def group_product(entries):
        picked = [(entry & 0xFFFF, entry >> 16) for entry in entries]
        rhs = jnp.concatenate([blocks_ref[spot] for _, spot in picked], axis=0)

        def lane_row(ref):
            halves = []
            for p in range(0, GROUP, 2):
                a = ref[pl.ds(picked[p][0], 1), :]
                b = ref[pl.ds(picked[p + 1][0], 1), :]
                halves.append(jnp.where(low_lane, a, b))
            return jnp.concatenate(halves, axis=1)

        left = lane_row(off_ref)
        right_w = lane_row(fx_ref).astype(F32) / 256.0
        lower_w = lane_row(fy_ref).astype(F32) / 256.0
        column = lax.broadcasted_iota(jnp.int32, (IMGW, GROUP * BLK), 0)
        across = jnp.where(column == left, 1.0 - right_w, 0.0) + jnp.where(
            column == left + 1, right_w, 0.0
        )
        band = jnp.concatenate([(1.0 - lower_w) * across, lower_w * across], axis=0).astype(BF16)
        return jnp.dot(band, rhs, preferred_element_type=F32)

    def overfill(out, at, inside):
        have = count_ref[at]

        @pl.when(have > GROUP)
        def _():
            acc_ref[...] = jnp.zeros_like(acc_ref)

            @pl.loop(0, (have + GROUP - 1) // GROUP)
            def _(m):
                entries = []
                for g in range(GROUP):
                    index = m * GROUP + g
                    entry = list_ref[at * wide + jnp.minimum(index, wide - 1)]
                    entries.append(jnp.where(index < have, entry, wide))
                acc_ref[...] = acc_ref[...] + group_product(entries)

            out[inside[0], inside[1]] = acc_ref[...].astype(BF16)

    inside = outs[0].shape[1]
    for chunk in range(2):
        for half in (1, 0):
            out = outs[2 * chunk + half]
            base = half * (slots // 2) * per + chunk * inside

            def visit(spot, base=base):
                place = spot // inside
                local = spot - place * inside
                return place, local, base + place * per + local

            @pl.loop(0, (slots // 2) * inside // BATCH)
            def _(m, out=out, visit=visit):
                found = []
                for n in range(BATCH):
                    place, local, at = visit(m * BATCH + n)
                    entries = [list_ref[at * wide + g] for g in range(GROUP)]
                    found.append((place, local, group_product(entries).astype(BF16)))
                for place, local, value in found:
                    out[place, local] = value

            @pl.loop(0, (slots // 2) * inside)
            def _(spot, out=out, visit=visit):
                place, local, at = visit(spot)
                overfill(out, at, (place, local))


def swap_low_bits(value):
    return (value & ~3) | ((value & 1) << 1) | ((value >> 1) & 1)


def slot_of(away, core, bits):
    place = 0
    first = jnp.where((core == 1) & (bits >= 2), swap_low_bits(away), away)
    for n in range(bits):
        place = place | (((first >> n) & 1) << (bits - 1 - n))
    return place


def warp_pieces(info, route, cells, cells_other, sources, tiles, per, edge, after):
    own = sources[0].shape[0] + sources[1].shape[0]
    chans = sources[0].shape[2]
    bits = int(math.log2(tiles)) - 1
    slots = tiles // 2
    shape = jax.ShapeDtypeStruct((slots // 2, per // 2, 2 * IMGW, chans), BF16)
    return pl.pallas_call(
        functools.partial(pieces_kernel, (own, per, bits, edge, len(after))),
        in_specs=[SMEM, SMEM, VMEM, VMEM] + [ANY] * (4 + len(after)),
        out_specs=[VMEM] * 4,
        out_shape=[shape] * 4,
        scratch_shapes=[
            pltpu.VMEM((2 * own, BLK, chans), BF16),
            pltpu.VMEM((3, 2 * own + 8, 2 * BLK), jnp.int32),
            pltpu.VMEM((2 * IMGW, chans), F32),
            pltpu.SMEM((slots * per,), jnp.int32),
            pltpu.SMEM((slots * per * 2 * own,), jnp.int32),
            pltpu.SemaphoreType.DMA((4,)),
        ],
        compiler_params=params(),
        cost_estimate=cost(
            2 * slots * per * 2 * IMGW * GROUP * BLK * chans, 2 * (own * 2 * BLK * chans + slots * per * 2 * IMGW * chans)
        ),
        name="warp_pieces",
    )(info, route, cells, cells_other, *sources, *after)


def slope_kernel(img_ref, w_ref, *refs):
    slope_ref = refs[-1]
    value = jnp.dot(img_ref[...], w_ref[...], preferred_element_type=F32)
    sigma = jax.nn.sigmoid(value)
    slope_ref[...] = sigma * (1.0 + value * (1.0 - sigma))


def image_slope(image, weight, after):
    pixels, chans = image.shape
    return pl.pallas_call(
        slope_kernel,
        in_specs=[VMEM, VMEM] + [ANY] * len(after),
        out_specs=VMEM,
        out_shape=jax.ShapeDtypeStruct((pixels, chans), F32),
        compiler_params=params(),
        cost_estimate=cost(2 * pixels * chans * chans, 10 * pixels * chans),
        name="image_slope",
    )(image, weight, *after)


def image_kernel(chunks, order_ref, *refs):
    terms = refs[: sum(chunks)]
    slope_ref, image_ref, w_ref, img_out, keep_ref, send_ref, wide_ref = refs[sum(chunks) :]
    feature = []
    start = 0
    for size in chunks:
        total = terms[start][0].astype(F32)
        for term in terms[start + 1 : start + size]:
            total = total + term[0].astype(F32)
        feature.append(total.reshape(-1, total.shape[-1]))
        start += size
    feature = jnp.concatenate(feature, axis=0)
    scaled = (feature * slope_ref[...]).astype(BF16)
    wide_ref[...] = tn_dot(image_ref[...], scaled)
    spread(wide_ref, order_ref, keep_ref, send_ref)
    img_out[...] = nt_dot(scaled, w_ref[...]).astype(BF16)


def image_layer(order, chunks, slope, image, weight):
    pixels, chans = slope.shape
    half = jax.ShapeDtypeStruct((1, chans // 2, chans), BF16)
    whole = lambda *shape: pl.BlockSpec(shape, lambda n: (0,) * len(shape))
    terms = [term for chunk in chunks for term in chunk]
    return pl.pallas_call(
        functools.partial(image_kernel, tuple(len(chunk) for chunk in chunks)),
        grid=(1,),
        in_specs=[SMEM]
        + [whole(1, *term.shape[1:]) for term in terms]
        + [whole(pixels, chans), whole(pixels, chans), whole(chans, chans)],
        out_specs=[whole(pixels, chans), whole(1, chans // 2, chans), whole(1, chans // 2, chans)],
        out_shape=[jax.ShapeDtypeStruct((pixels, chans), BF16), half, half],
        scratch_shapes=[pltpu.VMEM((chans, chans), F32)],
        compiler_params=params(),
        cost_estimate=cost(4 * pixels * chans * chans, 16 * pixels * chans),
        name="image_layer",
    )(order, *terms, slope, image, weight)


def exchange(value, size_dp, size_tile, flip):
    pairs = []
    for d in range(size_dp):
        for t in range(size_tile):
            dm, tm = flip(t & 1)
            pairs.append((d * size_tile + t, (d ^ dm) * size_tile + (t ^ tm)))
    return lax.ppermute(value, ("dp", "tile"), pairs)


def step_masks(size_dp, size_tile, core):
    dp_masks = [(1 << n, 0) for n in range(int(math.log2(size_dp)))]
    tile_masks = [(0, 1 << n) for n in range(1, int(math.log2(size_tile)))]
    masks = dp_masks + tile_masks
    if core == 1 and len(masks) >= 2:
        masks = [masks[1], masks[0]] + masks[2:]
    return masks


def part_order(me_dp, me_tile, size_dp, size_tile, levels):
    core = me_tile & 1
    kept = []
    for which in (0, 1):
        value = 0
        for dm, tm in step_masks(size_dp, size_tile, which)[: levels - 1]:
            bit = ((me_dp & dm) | (me_tile & tm)) != 0
            value = 2 * value + bit.astype(jnp.int32)
        kept.append(value)
    top = 1 << (levels - 1)
    places = jnp.arange(top, dtype=jnp.int32)
    same = (places ^ jnp.where(core == 0, kept[0], kept[1])) + core * top
    flipped = (places ^ jnp.where(core == 0, kept[1], kept[0])) + (1 - core) * top
    return jnp.concatenate([same, flipped])


def region_sum(terms, axis, low, high):
    total = lax.slice_in_dim(terms[0], low, high, axis=axis).astype(F32)
    for term in terms[1:]:
        total = total + lax.slice_in_dim(term, low, high, axis=axis).astype(F32)
    return total


class Chain:
    def __init__(self, keep, send, sizes, levels, scale):
        self.sizes = sizes
        self.masks = [step_masks(*sizes, core) for core in (0, 1)]
        self.steps = len(self.masks[0])
        self.levels = levels
        self.scale = scale
        self.terms = [keep]
        self.sent = send
        self.recv = None
        self.extent = keep.shape[1]
        self.count = 1 + self.steps + levels
        self.done = 0

    def total(self):
        if self.done <= self.levels:
            return region_sum(self.terms[:-1] + [self.recv], 1, 0, self.extent)
        return self.sent.astype(F32) + self.recv.astype(F32)

    def hold(self, *values):
        self.recv = together(self.recv, *values)[0]

    def step(self, *after):
        n = self.done
        which = n
        if n == 0:
            send = self.sent
        elif n < self.levels:
            self.terms[-1] = self.recv
            send = region_sum(self.terms, 1, self.extent // 2, self.extent).astype(BF16)
            self.extent //= 2
        elif n <= self.steps:
            send = self.total().astype(BF16)
        else:
            which = self.levels - (n - self.steps)
            if n == self.steps + 1:
                send = (self.total() * self.scale).astype(BF16)
            else:
                send = jnp.concatenate([self.sent, self.recv], axis=1)
        if after:
            send = together(send, *after)[0]
        flip = lambda core: (0, 1) if which == 0 else self.masks[core][which - 1]
        self.sent = send
        self.recv = exchange(send, *self.sizes, flip)
        if n < self.levels:
            self.terms.append(self.recv)
        self.done += 1

    def more(self):
        return self.done < self.count

    def tie(self, value):
        self.recv, value = together(self.recv, value)
        return value


def place_kernel(spans, *refs):
    tables = refs[: len(spans)]
    sources = refs[len(spans) : 3 * len(spans)]
    conv_ref, back_ref = refs[3 * len(spans) :]
    step = pl.program_id(0)
    start = 0
    for n, span in enumerate(spans):
        out_ref = back_ref if n == len(spans) - 1 else conv_ref
        parts = tables[n].shape[0]
        size = out_ref.shape[1] // parts

        @pl.when((step >= start) & (step < start + span))
        def _(n=n, out_ref=out_ref, parts=parts, size=size):
            for half in range(2):
                for s in range(parts // 2):
                    place = tables[n][half * (parts // 2) + s]
                    target = pl.multiple_of(place * size, size)
                    out_ref[:, pl.ds(target, size), :] = sources[2 * n + half][
                        :, s * size : (s + 1) * size, :
                    ]

        start += span


def place_parts(tables, chunks):
    chans = chunks[0][0].shape[2]
    spans = tuple(max(1, mine.shape[0] // 3) for mine, _ in chunks)
    starts = [sum(spans[:n]) for n in range(len(spans))]
    groups = sum(spans) - 1
    in_specs = [SMEM] * len(tables)
    for (mine, _), span, start in zip(chunks, spans, starts):
        block = (mine.shape[0] // span,) + mine.shape[1:]
        index = lambda t, span=span, start=start: (jnp.clip(t - start, 0, span - 1), 0, 0)
        in_specs += [pl.BlockSpec(block, index)] * 2
    return pl.pallas_call(
        functools.partial(place_kernel, spans),
        grid=(sum(spans),),
        in_specs=in_specs,
        out_specs=[
            pl.BlockSpec((3, chans, chans), lambda t: (jnp.minimum(t, groups - 1), 0, 0)),
            pl.BlockSpec((1, chans, chans), lambda t: (0, 0, 0)),
        ],
        out_shape=[
            jax.ShapeDtypeStruct((3 * groups, chans, chans), BF16),
            jax.ShapeDtypeStruct((1, chans, chans), BF16),
        ],
        compiler_params=params(),
        cost_estimate=cost(0, 40 * chans * chans),
        name="place_parts",
    )(*tables, *[half for chunk in chunks for half in chunk])


def together(*values):
    return lax.optimization_barrier(values)


def body(grad_out, bev_act, conv_weight, img_in, backbone_weight, route, offsets, frac_x, frac_y):
    tiles = lax.axis_size("tile")
    pods = lax.axis_size("dp")
    my_tile = lax.axis_index("tile")
    my_pod = lax.axis_index("dp")
    grad = grad_out[0]
    rows, cols, chans = grad.shape
    image = img_in[0]
    weight = jnp.transpose(conv_weight, (1, 2, 0, 3))
    per = image.shape[0] // (2 * IMGW)
    own = rows * cols // BLK
    edge_blocks = cols // BLK
    steps = int(math.log2(pods * tiles))
    most = min(steps, int(math.log2(chans // 16)))
    early_levels, late_levels, back_levels = (
        min(levels, most) for levels in (EARLY_LEVELS, LATE_LEVELS, BACK_LEVELS)
    )
    order_of = lambda levels: part_order(my_pod, my_tile, pods, tiles, levels)
    early_order, late_order, back_order = map(order_of, (early_levels, late_levels, back_levels))
    cell_scale = 1.0 / math.sqrt(pods * tiles * rows * cols)
    pixel_scale = 1.0 / math.sqrt(pods * tiles * image.shape[0])

    forward = [(i, i + 1) for i in range(tiles - 1)]
    backward = [(b, a) for a, b in forward]
    low = lax.ppermute(grad[rows - 1], "tile", forward)
    high = lax.ppermute(grad[0], "tile", backward)

    core_swap = [(t, t ^ 1) for t in range(tiles)]
    cells = jnp.stack([offsets[0], frac_x[0], frac_y[0]]).reshape(3, own, BLK)
    cells_other = lax.ppermute(cells, "tile", core_swap)

    info = jnp.reshape(my_tile, (1,)).astype(jnp.int32)
    inner = bev_rows(grad, [], weight, tuple(range(1, rows - 1)), [])
    inner_other = lax.ppermute(inner, "tile", core_swap)
    sizes = (pods, tiles)
    act = bev_act[0]
    edge = bev_rows(grad, [low, high], weight, (0, rows - 1), [inner, cells_other])
    edge_other = lax.ppermute(edge, "tile", core_swap)
    slope = image_slope(image, backbone_weight, [edge])
    as_blocks = lambda value: value.reshape(-1, BLK, chans)
    keep_a, send_a, keep_b, send_b = warp_pieces(
        info,
        route,
        cells,
        cells_other,
        [as_blocks(v) for v in (inner, edge, inner_other, edge_other)],
        tiles,
        per,
        edge_blocks,
        [slope],
    )

    tile_masks = [(0, 1 << n) for n in range(1, int(math.log2(tiles)))]
    swapped = [tile_masks[1], tile_masks[0]] + tile_masks[2:] if len(tile_masks) > 1 else tile_masks
    warp_masks = (tile_masks, swapped)

    def warp_step(terms, n, send):
        if n > 0:
            extent = keep_a.shape[0] >> (n - 1)
            send = region_sum(terms, 0, extent // 2, extent).astype(BF16)
        terms.append(exchange(send, *sizes, lambda core: warp_masks[core][n]))
        return send

    a, b = [keep_a], [keep_b]
    warp_step(a, 0, send_a)
    warp_step(b, 0, send_b)
    taps = tuple((i, j) for j in (1, 0, 2) for i in (1, 0, 2))
    groups = tuple(int(i == 2) for i, _ in taps)
    places = tuple(j if i == 2 else 3 * i + j for i, j in taps)
    keep_early, send_early, keep_late, send_late = wgrad(
        (early_order, late_order), act, grad, [low, high], taps, groups, places, [keep_a]
    )
    a[1], b[1], send_early, send_late = together(a[1], b[1], send_early, send_late)
    early = Chain(keep_early, send_early, sizes, early_levels, cell_scale)
    late = Chain(keep_late, send_late, sizes, late_levels, cell_scale)
    warp_step(a, 1, None)
    sent = warp_step(b, 1, None)
    early.step()
    late.step(sent)
    early.hold(a[2])
    sent = warp_step(a, 2, None)
    early.step(sent)
    late.hold(b[2])
    sent = warp_step(b, 2, None)
    late.step(sent)
    early.hold(a[3])
    early.step()
    for n in range(3, len(tile_masks)):
        for terms in (a, b):
            warp_step(terms, n, None)

    image_grad, keep_img, send_img = image_layer(back_order, [a, b], slope, image, backbone_weight)
    back = Chain(keep_img, send_img, sizes, back_levels, pixel_scale)
    early.step()
    late.step()
    early.recv, late.recv, _ = together(early.recv, late.recv, send_img)
    received = []
    for n in range(back.count):
        back.step()
        for chain, waits in ((early, EARLY_WAITS), (late, LATE_WAITS)):
            while chain.more() and waits[min(chain.done, len(waits) - 1)] <= n:
                wait = waits[min(chain.done, len(waits) - 1)]
                if wait > 0:
                    chain.hold(received[wait - 1])
                chain.step()
        received.append(back.recv)
    for chain in (early, late):
        while chain.more():
            chain.hold(received[-1])
            chain.step()

    conv_grad, backbone_grad = place_parts(
        [early_order, late_order, back_order],
        [(chain.sent, chain.recv) for chain in (early, late, back)],
    )
    backbone_grad = backbone_grad[0]
    conv_grad = jnp.transpose(conv_grad.reshape(3, 3, chans, chans), (2, 0, 1, 3))
    return (image_grad[None], conv_grad, backbone_grad)


def solution(mesh):
    return jax.shard_map(
        body,
        mesh=mesh,
        in_specs=(
            P("dp", "tile", None, None),
            P("dp", "tile", None, None),
            P(),
            P("dp", "tile", None),
            P(),
            P("dp", None),
            P("dp", "tile"),
            P("dp", "tile"),
            P("dp", "tile"),
        ),
        out_specs=(P("dp", "tile", None), P(), P()),
        check_vma=False,
    )
```

```python
import functools
import math

import jax
import jax.numpy as jnp
from jax import lax
from jax.experimental import pallas as pl
from jax.experimental.pallas import tpu as pltpu
from jax.sharding import PartitionSpec as P

BLK = 64
IMGW = 64
GROUP = 4
BATCH = 8
EARLY_LEVELS = 4
LATE_LEVELS = 3
BACK_LEVELS = 2
EARLY_WAITS = (0, 0, 0, 0, 0, 2, 3, 4, 6)
LATE_WAITS = (0, 0, 0, 0, 1, 3, 4, 6)
VMEM_BYTES = 63 * 1024 * 1024
F32 = jnp.float32
BF16 = jnp.bfloat16
VMEM = pl.BlockSpec(memory_space=pltpu.VMEM)
SMEM = pl.BlockSpec(memory_space=pltpu.SMEM)
ANY = pl.BlockSpec(memory_space=pl.ANY)


def params(**extra):
    return pltpu.CompilerParams(vmem_limit_bytes=VMEM_BYTES, **extra)


def cost(flops, nbytes):
    return pl.CostEstimate(flops=int(flops), bytes_accessed=int(nbytes), transcendentals=0)


def nt_dot(a, b):
    return lax.dot_general(a, b, (((1,), (1,)), ((), ())), preferred_element_type=F32)


def column_shift(value, by):
    if by == 0:
        return value
    length = value.shape[0]
    place = lax.broadcasted_iota(jnp.int32, value.shape, 0)
    edge = length - 1 if by > 0 else 0
    return jnp.where(place == edge, 0.0, pltpu.roll(value, (-by) % length, 0))


def bev_kernel(targets, halo, g_ref, *refs):
    if halo:
        low_ref, high_ref = refs[:2]
        refs = refs[2:]
    w_ref, out_ref, acc_ref = refs
    rows = g_ref.shape[0]
    step = pl.program_id(0)

    def frame(u):
        if u < 0:
            return low_ref[...]
        if u >= rows:
            return high_ref[...]
        return g_ref[u]

    for order, j in enumerate((1, 0, 2)):
        @pl.when(step == order)
        def _(j=j, order=order):
            rhs = jnp.concatenate([w_ref[i, 0] for i in range(3)], axis=1)
            for n, u in enumerate(targets):
                lhs = jnp.concatenate([frame(u - i + 1) for i in range(3)], axis=1)
                term = column_shift(nt_dot(lhs, rhs), 1 - j)
                if order == 0:
                    acc_ref[n] = term
                elif order == 1:
                    acc_ref[n] = acc_ref[n] + term
                else:
                    out_ref[n] = (acc_ref[n] + term).astype(BF16)


def col_tap(step):
    return jnp.where(step == 0, 1, jnp.where(step == 1, 0, 2))


def bev_rows(grad, halos, weight, targets, after):
    rows, cols, chans = grad.shape
    whole = lambda *shape: pl.BlockSpec(shape, lambda s: (0,) * len(shape))
    count = len(targets)

    def kernel(g_ref, *refs):
        n = len(halos) + 1
        bev_kernel(targets, len(halos) > 0, g_ref, *refs[:n], *refs[n + len(after) :])

    return pl.pallas_call(
        kernel,
        grid=(3,),
        in_specs=[whole(rows, cols, chans)]
        + [whole(cols, chans)] * len(halos)
        + [pl.BlockSpec((3, 1, chans, chans), lambda s: (0, col_tap(s), 0, 0))]
        + [ANY] * len(after),
        out_specs=whole(count, cols, chans),
        out_shape=jax.ShapeDtypeStruct((count, cols, chans), BF16),
        scratch_shapes=[pltpu.VMEM((count, cols, chans), F32)],
        compiler_params=params(),
        cost_estimate=cost(18 * count * cols * chans * chans, 2 * (2 * rows * cols * chans + 9 * chans * chans)),
        name="bev_rows",
    )(grad, *halos, weight, *after)


def tn_dot(a, b):
    return lax.dot_general(a, b, (((0,), (0,)), ((), ())), preferred_element_type=F32)


def spread(value_ref, order_ref, keep_ref, send_ref):
    parts = order_ref.shape[0]
    size = value_ref.shape[0] // parts
    for half, target in enumerate((keep_ref, send_ref)):
        for s in range(parts // 2):
            source = pl.multiple_of(order_ref[half * (parts // 2) + s] * size, size)
            target[0, s * size : (s + 1) * size, :] = value_ref[pl.ds(source, size), :].astype(BF16)


def wgrad_kernel(taps, groups, *refs):
    count = max(groups) + 1
    orders = refs[:count]
    a_ref, g_ref, low_ref, high_ref = refs[count : count + 4]
    outs = refs[-2 * count - 2 : -2]
    moved_ref, wide_ref = refs[-2:]
    rows, cols, chans = a_ref.shape
    total = rows * cols
    step = pl.program_id(0)
    for t, (i, j) in enumerate(taps):
        fresh = j != 1 and (t == 0 or taps[t - 1][1] != j)

        @pl.when(step == t)
        def _(i=i, j=j, fresh=fresh, group=groups[t]):
            if fresh:
                for u in range(rows):
                    moved_ref[u * cols : (u + 1) * cols, :] = column_shift(
                        a_ref[u].astype(F32), j - 1
                    ).astype(BF16)
            if j == 1:
                act = lambda low, high: a_ref[low:high].reshape((high - low) * cols, chans)
            else:
                act = lambda low, high: moved_ref[low * cols : high * cols, :]
            if i == 1:
                wide_ref[...] = tn_dot(act(0, rows), g_ref[...])
            elif i == 0:
                wide_ref[...] = tn_dot(act(0, rows - 1), g_ref[cols:, :]) + tn_dot(
                    act(rows - 1, rows), high_ref[...]
                )
            else:
                wide_ref[...] = tn_dot(act(1, rows), g_ref[: total - cols, :]) + tn_dot(
                    act(0, 1), low_ref[...]
                )
            spread(wide_ref, orders[group], *outs[2 * group : 2 * group + 2])


def pick(index, values):
    result = values[0]
    for n, value in enumerate(values):
        result = jnp.where(index == n, value, result)
    return result


def wgrad(orders, act, grad, halos, taps, groups, places, after):
    rows, cols, chans = grad.shape
    whole = lambda *shape: pl.BlockSpec(shape, lambda t: (0,) * len(shape))
    out_specs, out_shape = [], []
    for group in range(len(orders)):
        mine = [n for n in range(len(taps)) if groups[n] == group]
        visited = [places[max([n for n in mine if n <= t], default=mine[0])] for t in range(len(taps))]
        spec = pl.BlockSpec(
            (1, chans // 2, chans), lambda t, visited=visited: (pick(t, visited), 0, 0)
        )
        shape = jax.ShapeDtypeStruct((len(mine), chans // 2, chans), BF16)
        out_specs += [spec, spec]
        out_shape += [shape, shape]
    return pl.pallas_call(
        functools.partial(wgrad_kernel, taps, groups),
        grid=(len(taps),),
        in_specs=[SMEM] * len(orders)
        + [whole(rows, cols, chans), whole(rows * cols, chans)]
        + [whole(cols, chans)] * 2
        + [ANY] * len(after),
        out_specs=out_specs,
        out_shape=out_shape,
        scratch_shapes=[pltpu.VMEM((rows * cols, chans), BF16), pltpu.VMEM((chans, chans), F32)],
        compiler_params=params(),
        cost_estimate=cost(
            2 * len(taps) * rows * cols * chans * chans,
            2 * (2 * rows * cols * chans + len(taps) * chans * chans),
        ),
        name="wgrad",
    )(*orders, act, grad.reshape(rows * cols, chans), *halos, *after)


def pieces_kernel(
    plan, info_ref, route_ref, mine_ref, other_ref, *refs
):
    own_blocks, per, tile_bits, edge, after = plan
    sources = refs[:4]
    outs = refs[4 + after : 8 + after]
    blocks_ref, cells_ref, acc_ref, count_ref, list_ref, sems = refs[8 + after :]
    off_ref, fx_ref, fy_ref = cells_ref.at[0], cells_ref.at[1], cells_ref.at[2]
    copies = []
    start = 0
    for n, source in enumerate(sources):
        size = source.shape[0]
        copies.append(pltpu.make_async_copy(source, blocks_ref.at[pl.ds(start, size)], sems.at[n]))
        start += size
    for copy in copies:
        copy.start()
    for n in range(3):
        for start, cells in ((0, mine_ref), (own_blocks, other_ref)):
            cells_ref[n, start : start + own_blocks, :] = jnp.concatenate([cells[n], cells[n]], axis=1)
    tile = info_ref[0]
    core = tile & 1
    slots = outs[0].shape[0] * 2
    wide = 2 * own_blocks
    inner = own_blocks - 2 * edge

    @pl.loop(0, slots * per)
    def _(n):
        count_ref[n] = 0
        for g in range(GROUP):
            list_ref[n * wide + g] = wide

    per_bits = int(math.log2(per))
    for other in range(2):
        for first, last, shift in (
            (0, edge, inner),
            (edge, own_blocks - edge, -edge),
            (own_blocks - edge, own_blocks, 0),
        ):
            @pl.loop(first, last)
            def _(k, other=other, shift=shift):
                ident = route_ref[0, (tile ^ other) * own_blocks + k]
                owner = ident >> per_bits
                local = ident & (per - 1)

                @pl.when(((owner ^ tile) & 1) == 0)
                def _():
                    at = slot_of((owner ^ tile) >> 1, core, tile_bits) * per + local
                    have = count_ref[at]
                    spot = other * own_blocks + shift + k
                    list_ref[at * wide + have] = (spot << 16) + (other * own_blocks + k)
                    count_ref[at] = have + 1

    cells_ref[0, wide : wide + 8, :] = jnp.full((8, 2 * BLK), -2 * IMGW, jnp.int32)
    for n in range(1, 3):
        cells_ref[n, wide : wide + 8, :] = jnp.zeros((8, 2 * BLK), jnp.int32)

    for copy in copies:
        copy.wait()

    lanes = lax.broadcasted_iota(jnp.int32, (1, 2 * BLK), 1)
    low_lane = lanes < BLK

    def group_product(entries):
        picked = [(entry & 0xFFFF, entry >> 16) for entry in entries]
        rhs = jnp.concatenate([blocks_ref[spot] for _, spot in picked], axis=0)

        def lane_row(ref):
            halves = []
            for p in range(0, GROUP, 2):
                a = ref[pl.ds(picked[p][0], 1), :]
                b = ref[pl.ds(picked[p + 1][0], 1), :]
                halves.append(jnp.where(low_lane, a, b))
            return jnp.concatenate(halves, axis=1)

        left = lane_row(off_ref)
        right_w = lane_row(fx_ref).astype(F32) / 256.0
        lower_w = lane_row(fy_ref).astype(F32) / 256.0
        column = lax.broadcasted_iota(jnp.int32, (IMGW, GROUP * BLK), 0)
        across = jnp.where(column == left, 1.0 - right_w, 0.0) + jnp.where(
            column == left + 1, right_w, 0.0
        )
        band = jnp.concatenate([(1.0 - lower_w) * across, lower_w * across], axis=0).astype(BF16)
        return jnp.dot(band, rhs, preferred_element_type=F32)

    def overfill(out, at, inside):
        have = count_ref[at]

        @pl.when(have > GROUP)
        def _():
            acc_ref[...] = jnp.zeros_like(acc_ref)

            @pl.loop(0, (have + GROUP - 1) // GROUP)
            def _(m):
                entries = []
                for g in range(GROUP):
                    index = m * GROUP + g
                    entry = list_ref[at * wide + jnp.minimum(index, wide - 1)]
                    entries.append(jnp.where(index < have, entry, wide))
                acc_ref[...] = acc_ref[...] + group_product(entries)

            out[inside[0], inside[1]] = acc_ref[...].astype(BF16)

    inside = outs[0].shape[1]
    for chunk in range(2):
        for half in (1, 0):
            out = outs[2 * chunk + half]
            base = half * (slots // 2) * per + chunk * inside

            def visit(spot, base=base):
                place = spot // inside
                local = spot - place * inside
                return place, local, base + place * per + local

            @pl.loop(0, (slots // 2) * inside // BATCH)
            def _(m, out=out, visit=visit):
                found = []
                for n in range(BATCH):
                    place, local, at = visit(m * BATCH + n)
                    entries = [list_ref[at * wide + g] for g in range(GROUP)]
                    found.append((place, local, group_product(entries).astype(BF16)))
                for place, local, value in found:
                    out[place, local] = value

            @pl.loop(0, (slots // 2) * inside)
            def _(spot, out=out, visit=visit):
                place, local, at = visit(spot)
                overfill(out, at, (place, local))


def swap_low_bits(value):
    return (value & ~3) | ((value & 1) << 1) | ((value >> 1) & 1)


def slot_of(away, core, bits):
    place = 0
    first = jnp.where((core == 1) & (bits >= 2), swap_low_bits(away), away)
    for n in range(bits):
        place = place | (((first >> n) & 1) << (bits - 1 - n))
    return place


def warp_pieces(info, route, cells, cells_other, sources, tiles, per, edge, after):
    own = sources[0].shape[0] + sources[1].shape[0]
    chans = sources[0].shape[2]
    bits = int(math.log2(tiles)) - 1
    slots = tiles // 2
    shape = jax.ShapeDtypeStruct((slots // 2, per // 2, 2 * IMGW, chans), BF16)
    return pl.pallas_call(
        functools.partial(pieces_kernel, (own, per, bits, edge, len(after))),
        in_specs=[SMEM, SMEM, VMEM, VMEM] + [ANY] * (4 + len(after)),
        out_specs=[VMEM] * 4,
        out_shape=[shape] * 4,
        scratch_shapes=[
            pltpu.VMEM((2 * own, BLK, chans), BF16),
            pltpu.VMEM((3, 2 * own + 8, 2 * BLK), jnp.int32),
            pltpu.VMEM((2 * IMGW, chans), F32),
            pltpu.SMEM((slots * per,), jnp.int32),
            pltpu.SMEM((slots * per * 2 * own,), jnp.int32),
            pltpu.SemaphoreType.DMA((4,)),
        ],
        compiler_params=params(),
        cost_estimate=cost(
            2 * slots * per * 2 * IMGW * GROUP * BLK * chans, 2 * (own * 2 * BLK * chans + slots * per * 2 * IMGW * chans)
        ),
        name="warp_pieces",
    )(info, route, cells, cells_other, *sources, *after)


def slope_kernel(img_ref, w_ref, *refs):
    slope_ref = refs[-1]
    value = jnp.dot(img_ref[...], w_ref[...], preferred_element_type=F32)
    sigma = jax.nn.sigmoid(value)
    slope_ref[...] = sigma * (1.0 + value * (1.0 - sigma))


def image_slope(image, weight, after):
    pixels, chans = image.shape
    return pl.pallas_call(
        slope_kernel,
        in_specs=[VMEM, VMEM] + [ANY] * len(after),
        out_specs=VMEM,
        out_shape=jax.ShapeDtypeStruct((pixels, chans), F32),
        compiler_params=params(),
        cost_estimate=cost(2 * pixels * chans * chans, 10 * pixels * chans),
        name="image_slope",
    )(image, weight, *after)


def image_kernel(chunks, order_ref, *refs):
    terms = refs[: sum(chunks)]
    slope_ref, image_ref, w_ref, img_out, keep_ref, send_ref, wide_ref = refs[sum(chunks) :]
    feature = []
    start = 0
    for size in chunks:
        total = terms[start][0].astype(F32)
        for term in terms[start + 1 : start + size]:
            total = total + term[0].astype(F32)
        feature.append(total.reshape(-1, total.shape[-1]))
        start += size
    feature = jnp.concatenate(feature, axis=0)
    scaled = (feature * slope_ref[...]).astype(BF16)
    wide_ref[...] = tn_dot(image_ref[...], scaled)
    spread(wide_ref, order_ref, keep_ref, send_ref)
    img_out[...] = nt_dot(scaled, w_ref[...]).astype(BF16)


def image_layer(order, chunks, slope, image, weight):
    pixels, chans = slope.shape
    half = jax.ShapeDtypeStruct((1, chans // 2, chans), BF16)
    whole = lambda *shape: pl.BlockSpec(shape, lambda n: (0,) * len(shape))
    terms = [term for chunk in chunks for term in chunk]
    return pl.pallas_call(
        functools.partial(image_kernel, tuple(len(chunk) for chunk in chunks)),
        grid=(1,),
        in_specs=[SMEM]
        + [whole(1, *term.shape[1:]) for term in terms]
        + [whole(pixels, chans), whole(pixels, chans), whole(chans, chans)],
        out_specs=[whole(pixels, chans), whole(1, chans // 2, chans), whole(1, chans // 2, chans)],
        out_shape=[jax.ShapeDtypeStruct((pixels, chans), BF16), half, half],
        scratch_shapes=[pltpu.VMEM((chans, chans), F32)],
        compiler_params=params(),
        cost_estimate=cost(4 * pixels * chans * chans, 16 * pixels * chans),
        name="image_layer",
    )(order, *terms, slope, image, weight)


def exchange(value, size_dp, size_tile, flip):
    pairs = []
    for d in range(size_dp):
        for t in range(size_tile):
            dm, tm = flip(t & 1)
            pairs.append((d * size_tile + t, (d ^ dm) * size_tile + (t ^ tm)))
    return lax.ppermute(value, ("dp", "tile"), pairs)


def step_masks(size_dp, size_tile, core):
    dp_masks = [(1 << n, 0) for n in range(int(math.log2(size_dp)))]
    tile_masks = [(0, 1 << n) for n in range(1, int(math.log2(size_tile)))]
    masks = dp_masks + tile_masks
    if core == 1 and len(masks) >= 2:
        masks = [masks[1], masks[0]] + masks[2:]
    return masks


def part_order(me_dp, me_tile, size_dp, size_tile, levels):
    core = me_tile & 1
    kept = []
    for which in (0, 1):
        value = 0
        for dm, tm in step_masks(size_dp, size_tile, which)[: levels - 1]:
            bit = ((me_dp & dm) | (me_tile & tm)) != 0
            value = 2 * value + bit.astype(jnp.int32)
        kept.append(value)
    top = 1 << (levels - 1)
    places = jnp.arange(top, dtype=jnp.int32)
    same = (places ^ jnp.where(core == 0, kept[0], kept[1])) + core * top
    flipped = (places ^ jnp.where(core == 0, kept[1], kept[0])) + (1 - core) * top
    return jnp.concatenate([same, flipped])


def region_sum(terms, axis, low, high):
    total = lax.slice_in_dim(terms[0], low, high, axis=axis).astype(F32)
    for term in terms[1:]:
        total = total + lax.slice_in_dim(term, low, high, axis=axis).astype(F32)
    return total


class Chain:
    def __init__(self, keep, send, sizes, levels, scale):
        self.sizes = sizes
        self.masks = [step_masks(*sizes, core) for core in (0, 1)]
        self.steps = len(self.masks[0])
        self.levels = levels
        self.scale = scale
        self.terms = [keep]
        self.sent = send
        self.recv = None
        self.extent = keep.shape[1]
        self.count = 1 + self.steps + levels
        self.done = 0

    def total(self):
        if self.done <= self.levels:
            return region_sum(self.terms[:-1] + [self.recv], 1, 0, self.extent)
        return self.sent.astype(F32) + self.recv.astype(F32)

    def hold(self, *values):
        self.recv = together(self.recv, *values)[0]

    def step(self, *after):
        n = self.done
        which = n
        if n == 0:
            send = self.sent
        elif n < self.levels:
            self.terms[-1] = self.recv
            send = region_sum(self.terms, 1, self.extent // 2, self.extent).astype(BF16)
            self.extent //= 2
        elif n <= self.steps:
            send = self.total().astype(BF16)
        else:
            which = self.levels - (n - self.steps)
            if n == self.steps + 1:
                send = (self.total() * self.scale).astype(BF16)
            else:
                send = jnp.concatenate([self.sent, self.recv], axis=1)
        if after:
            send = together(send, *after)[0]
        flip = lambda core: (0, 1) if which == 0 else self.masks[core][which - 1]
        self.sent = send
        self.recv = exchange(send, *self.sizes, flip)
        if n < self.levels:
            self.terms.append(self.recv)
        self.done += 1

    def more(self):
        return self.done < self.count

    def tie(self, value):
        self.recv, value = together(self.recv, value)
        return value


def place_kernel(spans, *refs):
    tables = refs[: len(spans)]
    sources = refs[len(spans) : 3 * len(spans)]
    conv_ref, back_ref = refs[3 * len(spans) :]
    step = pl.program_id(0)
    start = 0
    for n, span in enumerate(spans):
        out_ref = back_ref if n == len(spans) - 1 else conv_ref
        parts = tables[n].shape[0]
        size = out_ref.shape[1] // parts

        @pl.when((step >= start) & (step < start + span))
        def _(n=n, out_ref=out_ref, parts=parts, size=size):
            for half in range(2):
                for s in range(parts // 2):
                    place = tables[n][half * (parts // 2) + s]
                    target = pl.multiple_of(place * size, size)
                    out_ref[:, pl.ds(target, size), :] = sources[2 * n + half][
                        :, s * size : (s + 1) * size, :
                    ]

        start += span


def place_parts(tables, chunks):
    chans = chunks[0][0].shape[2]
    spans = tuple(max(1, mine.shape[0] // 3) for mine, _ in chunks)
    starts = [sum(spans[:n]) for n in range(len(spans))]
    groups = sum(spans) - 1
    in_specs = [SMEM] * len(tables)
    for (mine, _), span, start in zip(chunks, spans, starts):
        block = (mine.shape[0] // span,) + mine.shape[1:]
        index = lambda t, span=span, start=start: (jnp.clip(t - start, 0, span - 1), 0, 0)
        in_specs += [pl.BlockSpec(block, index)] * 2
    return pl.pallas_call(
        functools.partial(place_kernel, spans),
        grid=(sum(spans),),
        in_specs=in_specs,
        out_specs=[
            pl.BlockSpec((3, chans, chans), lambda t: (jnp.minimum(t, groups - 1), 0, 0)),
            pl.BlockSpec((1, chans, chans), lambda t: (0, 0, 0)),
        ],
        out_shape=[
            jax.ShapeDtypeStruct((3 * groups, chans, chans), BF16),
            jax.ShapeDtypeStruct((1, chans, chans), BF16),
        ],
        compiler_params=params(),
        cost_estimate=cost(0, 40 * chans * chans),
        name="place_parts",
    )(*tables, *[half for chunk in chunks for half in chunk])


def together(*values):
    return lax.optimization_barrier(values)


def body(grad_out, bev_act, conv_weight, img_in, backbone_weight, route, offsets, frac_x, frac_y):
    tiles = lax.axis_size("tile")
    pods = lax.axis_size("dp")
    my_tile = lax.axis_index("tile")
    my_pod = lax.axis_index("dp")
    grad = grad_out[0]
    rows, cols, chans = grad.shape
    image = img_in[0]
    weight = jnp.transpose(conv_weight, (1, 2, 0, 3))
    per = image.shape[0] // (2 * IMGW)
    own = rows * cols // BLK
    edge_blocks = cols // BLK
    steps = int(math.log2(pods * tiles))
    most = min(steps, int(math.log2(chans // 16)))
    early_levels, late_levels, back_levels = (
        min(levels, most) for levels in (EARLY_LEVELS, LATE_LEVELS, BACK_LEVELS)
    )
    order_of = lambda levels: part_order(my_pod, my_tile, pods, tiles, levels)
    early_order, late_order, back_order = map(order_of, (early_levels, late_levels, back_levels))
    cell_scale = 1.0 / math.sqrt(pods * tiles * rows * cols)
    pixel_scale = 1.0 / math.sqrt(pods * tiles * image.shape[0])

    forward = [(i, i + 1) for i in range(tiles - 1)]
    backward = [(b, a) for a, b in forward]
    low = lax.ppermute(grad[rows - 1], "tile", forward)
    high = lax.ppermute(grad[0], "tile", backward)

    core_swap = [(t, t ^ 1) for t in range(tiles)]
    cells = jnp.stack([offsets[0], frac_x[0], frac_y[0]]).reshape(3, own, BLK)
    cells_other = lax.ppermute(cells, "tile", core_swap)

    info = jnp.reshape(my_tile, (1,)).astype(jnp.int32)
    inner = bev_rows(grad, [], weight, tuple(range(1, rows - 1)), [])
    inner_other = lax.ppermute(inner, "tile", core_swap)
    sizes = (pods, tiles)
    act = bev_act[0]
    edge = bev_rows(grad, [low, high], weight, (0, rows - 1), [inner, cells_other])
    edge_other = lax.ppermute(edge, "tile", core_swap)
    slope = image_slope(image, backbone_weight, [edge])
    as_blocks = lambda value: value.reshape(-1, BLK, chans)
    keep_a, send_a, keep_b, send_b = warp_pieces(
        info,
        route,
        cells,
        cells_other,
        [as_blocks(v) for v in (inner, edge, inner_other, edge_other)],
        tiles,
        per,
        edge_blocks,
        [slope],
    )

    tile_masks = [(0, 1 << n) for n in range(1, int(math.log2(tiles)))]
    swapped = [tile_masks[1], tile_masks[0]] + tile_masks[2:] if len(tile_masks) > 1 else tile_masks
    warp_masks = (tile_masks, swapped)

    def warp_step(terms, n, send):
        if n > 0:
            extent = keep_a.shape[0] >> (n - 1)
            send = region_sum(terms, 0, extent // 2, extent).astype(BF16)
        terms.append(exchange(send, *sizes, lambda core: warp_masks[core][n]))
        return send

    a, b = [keep_a], [keep_b]
    warp_step(a, 0, send_a)
    warp_step(b, 0, send_b)
    taps = tuple((i, j) for j in (1, 0, 2) for i in (1, 0, 2))
    groups = tuple(int(i == 2) for i, _ in taps)
    places = tuple(j if i == 2 else 3 * i + j for i, j in taps)
    keep_early, send_early, keep_late, send_late = wgrad(
        (early_order, late_order), act, grad, [low, high], taps, groups, places, [keep_a]
    )
    a[1], b[1], send_early, send_late = together(a[1], b[1], send_early, send_late)
    early = Chain(keep_early, send_early, sizes, early_levels, cell_scale)
    late = Chain(keep_late, send_late, sizes, late_levels, cell_scale)
    warp_step(a, 1, None)
    sent = warp_step(b, 1, None)
    early.step()
    late.step(sent)
    early.hold(a[2])
    sent = warp_step(a, 2, None)
    early.step(sent)
    late.hold(b[2])
    sent = warp_step(b, 2, None)
    late.step(sent)
    early.hold(a[3])
    early.step()
    for n in range(3, len(tile_masks)):
        for terms in (a, b):
            warp_step(terms, n, None)

    image_grad, keep_img, send_img = image_layer(back_order, [a, b], slope, image, backbone_weight)
    back = Chain(keep_img, send_img, sizes, back_levels, pixel_scale)
    early.step()
    late.step()
    early.recv, late.recv, _ = together(early.recv, late.recv, send_img)
    received = []
    for n in range(back.count):
        back.step()
        for chain, waits in ((early, EARLY_WAITS), (late, LATE_WAITS)):
            while chain.more() and waits[min(chain.done, len(waits) - 1)] <= n:
                wait = waits[min(chain.done, len(waits) - 1)]
                if wait > 0:
                    chain.hold(received[wait - 1])
                chain.step()
        received.append(back.recv)
    for chain in (early, late):
        while chain.more():
            chain.hold(received[-1])
            chain.step()

    conv_grad, backbone_grad = place_parts(
        [early_order, late_order, back_order],
        [(chain.sent, chain.recv) for chain in (early, late, back)],
    )
    backbone_grad = backbone_grad[0]
    conv_grad = jnp.transpose(conv_grad.reshape(3, 3, chans, chans), (2, 0, 1, 3))
    return (image_grad[None], conv_grad, backbone_grad)


def solution(mesh):
    return jax.shard_map(
        body,
        mesh=mesh,
        in_specs=(
            P("dp", "tile", None, None),
            P("dp", "tile", None, None),
            P(),
            P("dp", "tile", None),
            P(),
            P("dp", None),
            P("dp", "tile"),
            P("dp", "tile"),
            P("dp", "tile"),
        ),
        out_specs=(P("dp", "tile", None), P(), P()),
        check_vma=False,
    )
```
